256 devices in a mesh: doc: 16 (over z_lo, x), head: 8 (over z_hi, y), cuts: 2 (over core).
Axes of the slice: x: 4, y: 4, z: 8 (z_hi: 2, z_lo: 4; z = z_hi * 4 + z_lo), core: 2. Of those that a mesh axis runs over, the one named last changes fastest.
Arguments:
- inputs: bfloat16 [2, 16, 256, 4096], P('cuts', 'doc'), may hold values from -9 to 9
- weight_query: bfloat16 [4096, 2048], P(None, 'head'), may hold values from -1 to 1
- weight_key: bfloat16 [4096, 2048], P(None, 'head'), may hold values from -2 to 2
- weight_value: bfloat16 [4096, 2048], P(None, 'head'), may hold values from -0.09375 to 0.09375
- grad_output: bfloat16 [2, 16, 256, 2048], P('cuts', 'doc', None, 'head'), may hold values from -24 to 24
- partner_one: int32 [2, 16], P('cuts'), may hold values from 0 to 15, each once within a row
- partner_two: int32 [2, 16], P('cuts'), may hold values from 0 to 15, each once within a row
Outputs:
- grad_key: bfloat16 [2, 16, 256, 2048], P('cuts', 'doc', None, 'head')
- grad_value: bfloat16 [2, 16, 256, 2048], P('cuts', 'doc', None, 'head')
- grad_weight_query: float32 [4096, 2048], P(('doc', 'cuts'), 'head')
- grad_weight_key: float32 [4096, 2048], P(('doc', 'cuts'), 'head')
- grad_weight_value: float32 [4096, 2048], P(('doc', 'cuts'), 'head')
- grad_input: bfloat16 [2, 16, 4096, 256], P('cuts', 'doc', 'head')
The draws below stay inside these ranges and needn't reach their ends.
Inputs may be any that keep to these rules, and one draw needn't show every extreme that they name: `partner_one`: each row is a permutation of the documents 0 to 15 of the slice. `partner_two`: each row is a permutation of the documents 0 to 15 of the slice.
All inputs are finite; a program needn't handle non-finite values.
Results may differ from the reference program's by a relative error of at most 0.033.
Values may be sent and summed in bfloat16 or wider, within the bound.
No kernel may reach another device: no remote copies, remote signals or barrier semaphores. Data moves between devices by JAX's collectives and lax.ppermute only.
A program may use at most 128 MiB of HBM per device.

```python
import math
import jax
import jax.numpy as jnp
from jax import lax

D = 4096
HD = 128
TOK = 256
HEADS = 16
DOCS = 16
SLICES = 2


def draw_inputs(key, part):
    full_shape = (SLICES, DOCS, TOK, D)
    drawn = jnp.clip(jax.random.normal(jax.random.fold_in(key, 3), full_shape, jnp.float32), -6.0, 6.0)
    return drawn.astype(jnp.bfloat16)


def shared_query(key):
    drawn = jax.random.normal(jax.random.fold_in(key, 7), (D, HEADS * HD), jnp.float32)
    return jnp.clip(drawn, -6.0, 6.0) / math.sqrt(D)


def draw_weight_query(key, part):
    return shared_query(key).astype(jnp.bfloat16)


def draw_weight_key(key, part):
    drawn = jnp.clip(jax.random.normal(jax.random.fold_in(key, 9), (D, HEADS * HD), jnp.float32), -6.0, 6.0) / math.sqrt(D)
    return drawn.astype(jnp.bfloat16)


def levels(key, shape, shards, smallest, high):
    loudness = 1.0
    for dim, shards_of in shards:
        draws = jax.random.uniform(jax.random.fold_in(jax.random.fold_in(key, 6), dim), (shards_of,), jnp.float32, smallest / len(shards), high / len(shards))
        loudness = loudness * jnp.repeat(jnp.exp(draws), shape[dim] // shards_of).reshape((-1,) + (1,) * (len(shape) - 1 - dim))
    return loudness


def centred(own_key, extent, width, reach, split=(), kind=jnp.bfloat16):
    array = width * jax.random.normal(own_key, extent, jnp.float32)
    if split:
        array = array * levels(own_key, extent, split, -0.22, 0.18)
    return jnp.clip(array, -reach, reach).astype(kind)


def setup_inputs(seed: int = 0) -> dict:
    arg_keys = jax.random.split(jax.random.key(seed), 8)
    inputs = draw_inputs(jax.random.fold_in(arg_keys[7], 71), 0)
    weight_query = draw_weight_query(jax.random.fold_in(arg_keys[7], 71), 0)
    weight_key = draw_weight_key(jax.random.fold_in(arg_keys[7], 71), 0)
    weight_value = centred(arg_keys[3], (D, HEADS * HD), D ** -0.5, 0.09375, ((1, 8),))
    grad_output = centred(arg_keys[4], (SLICES, DOCS, TOK, HEADS * HD), 4.0, 24.0, ((0, 2), (1, 16), (3, 8)))
    partner_one = jax.vmap(lambda own: jax.random.permutation(own, DOCS))(jax.random.split(arg_keys[5], SLICES)).reshape((SLICES, DOCS)).astype(jnp.int32)
    partner_two = jax.vmap(lambda own: jax.random.permutation(own, DOCS))(jax.random.split(arg_keys[6], SLICES)).reshape((SLICES, DOCS)).astype(jnp.int32)
    return dict(inputs=inputs, weight_query=weight_query, weight_key=weight_key, weight_value=weight_value, grad_output=grad_output, partner_one=partner_one, partner_two=partner_two)


def attend(bundle):
    query_heads, keys_all, values_all, dout_heads = bundle
    length = query_heads.shape[0]
    factor = 1.0 / math.sqrt(HD)
    query_wide = query_heads.astype(jnp.float32)
    keys_wide = keys_all.astype(jnp.float32)
    values_wide = values_all.astype(jnp.float32)
    dout_wide = dout_heads.astype(jnp.float32)
    scores = jnp.einsum('qhe,khe->hqk', query_wide, keys_wide) * factor
    row_index = lax.broadcasted_iota(jnp.int32, (length, 3 * length), 0)
    col_index = lax.broadcasted_iota(jnp.int32, (length, 3 * length), 1)
    allowed = (col_index >= length) | (col_index <= row_index)
    scores = jnp.where(allowed[None], scores, -jnp.inf)
    maximum = lax.optimization_barrier(jnp.max(scores, axis=-1, keepdims=True))
    exponent = jnp.exp(scores - maximum)
    totals = lax.optimization_barrier(jnp.sum(exponent, axis=-1, keepdims=True))
    probability = exponent / totals
    rounded = lax.optimization_barrier(probability.astype(jnp.bfloat16)).astype(jnp.float32)
    attended = jnp.einsum('hqk,khe->qhe', rounded, values_wide)
    row_delta = lax.optimization_barrier(jnp.sum(dout_wide * attended, axis=-1))
    prob_grad = jnp.einsum('qhe,khe->hqk', dout_wide, values_wide)
    score_grad = probability * (prob_grad - row_delta.T[:, :, None])
    score_grad = lax.optimization_barrier(score_grad.astype(jnp.bfloat16)).astype(jnp.float32)
    grad_query = jnp.einsum('hqk,khe->qhe', score_grad, keys_wide) * factor
    grad_keys = jnp.einsum('hqk,qhe->khe', score_grad, query_wide) * factor
    grad_values = jnp.einsum('hqk,qhe->khe', rounded, dout_wide)
    return (grad_query, grad_keys, grad_values)

def select_rows(array_in, indices):
    return jnp.take(array_in, indices, axis=0)

def reference(inputs, weight_query, weight_key, weight_value, grad_output, partner_one, partner_two):
    columns = HEADS * HD
    doc_total = SLICES * DOCS
    flattened = inputs.reshape(doc_total * TOK, D)

    def project(weights):
        product = jnp.dot(flattened, weights, preferred_element_type=jnp.float32)
        return product.astype(jnp.bfloat16).reshape(SLICES, DOCS, TOK, columns)
    queries = project(weight_query)
    keys = project(weight_key)
    values = project(weight_value)
    select_docs = jax.vmap(select_rows)
    keys_all = jnp.concatenate([keys, select_docs(keys, partner_one), select_docs(keys, partner_two)], axis=2)
    values_all = jnp.concatenate([values, select_docs(values, partner_one), select_docs(values, partner_two)], axis=2)
    per_doc = (queries.reshape(doc_total, TOK, HEADS, HD), keys_all.reshape(doc_total, 3 * TOK, HEADS, HD), values_all.reshape(doc_total, 3 * TOK, HEADS, HD), grad_output.reshape(doc_total, TOK, HEADS, HD))
    grad_query, grad_keys, grad_values = lax.map(attend, per_doc)
    grad_query = grad_query.reshape(SLICES, DOCS, TOK, columns).astype(jnp.bfloat16)
    grad_keys = grad_keys.reshape(SLICES, DOCS, 3 * TOK, columns)
    grad_values = grad_values.reshape(SLICES, DOCS, 3 * TOK, columns)

    def settle(terms):
        summed = terms[:, :, :TOK]
        for slice_index in range(SLICES):
            summed = summed.at[slice_index, partner_one[slice_index].astype(jnp.int32)].add(terms[slice_index, :, TOK:2 * TOK])
            summed = summed.at[slice_index, partner_two[slice_index].astype(jnp.int32)].add(terms[slice_index, :, 2 * TOK:])
        return summed
    grad_key = settle(grad_keys).astype(jnp.bfloat16)
    grad_value = settle(grad_values).astype(jnp.bfloat16)
    all_grads = jnp.concatenate([grad_query, grad_key, grad_value], axis=-1).reshape(doc_total, TOK, 3 * columns)
    docs_inputs = inputs.reshape(doc_total, TOK, D)

    def accumulate(summed, pair_in):
        doc_inputs, doc_grads = pair_in
        product = jnp.dot(doc_inputs.T, doc_grads, preferred_element_type=jnp.float32)
        product = lax.optimization_barrier(product.astype(jnp.bfloat16)).astype(jnp.float32)
        return (summed + product, None)
    summed, unused = lax.scan(accumulate, jnp.zeros((D, 3 * columns), jnp.float32), (docs_inputs, all_grads))
    combined = jnp.concatenate([weight_query, weight_key, weight_value], axis=1)
    grad_input = jnp.dot(all_grads.reshape(doc_total * TOK, 3 * columns), combined.T, preferred_element_type=jnp.float32)
    grad_input = grad_input.astype(jnp.bfloat16).reshape(SLICES, DOCS, TOK, D).transpose(0, 1, 3, 2)
    return (grad_key, grad_value, summed[:, :columns], summed[:, columns:2 * columns], summed[:, 2 * columns:], grad_input)
```

```python
import functools
import math

import jax
import jax.numpy as jnp
from jax import lax
from jax.experimental import pallas as pl
from jax.experimental.pallas import tpu as pltpu
from jax.sharding import PartitionSpec as P

HD = 128
XS = 4
ZS = 4
YS = 4
BF = jnp.bfloat16
F32 = jnp.float32
SMALL = 16 * 1024 * 1024
LARGE = 52 * 1024 * 1024
VMEM = pl.BlockSpec(memory_space=pltpu.VMEM)
SMEM = pl.BlockSpec(memory_space=pltpu.SMEM)
ANY = pl.BlockSpec(memory_space=pl.ANY)


def _params(limit):
    return pltpu.CompilerParams(vmem_limit_bytes=limit)


def _cost(flops, nbytes, trans=0):
    return pl.CostEstimate(flops=flops, bytes_accessed=nbytes, transcendentals=trans)


def _nt(a, b):
    return lax.dot_general(a, b, (((1,), (1,)), ((), ())), preferred_element_type=F32)


def _nn(a, b):
    return lax.dot_general(a, b, (((1,), (0,)), ((), ())), preferred_element_type=F32)


def _tn(a, b):
    return lax.dot_general(a, b, (((0,), (0,)), ((), ())), preferred_element_type=F32)


PIECES = 8
HINT = 30_000_000_000


def _project_body(x_ref, wq_ref, wk_ref, wv_ref, do_ref, o_ref, *rest):
    outs, (xs, ws, acc, sems) = rest[:XS], rest[XS:]
    d, n = wq_ref.shape
    my_x = lax.rem(lax.axis_index("doc"), XS)
    width = d // (ZS * XS)
    kb = d // PIECES
    last = pltpu.make_async_copy(do_ref, o_ref.at[:, 3 * n :], sems.at[PIECES, 0])
    copies = []
    for i in range(PIECES):
        part = slice(i * kb, (i + 1) * kb)
        row = [pltpu.make_async_copy(x_ref.at[:, part], xs.at[:, part], sems.at[i, 0])]
        for j, w in enumerate((wq_ref, wk_ref, wv_ref)):
            row.append(pltpu.make_async_copy(w.at[part, :], ws.at[j, part, :], sems.at[i, j + 1]))
        for c in row:
            c.start()
        copies.append(row)
    last.start()
    for i in range(PIECES):
        part = slice(i * kb, (i + 1) * kb)
        for c in copies[i]:
            c.wait()
        x = xs[:, part]
        for j in range(3):
            cols = slice(j * n, (j + 1) * n)
            prod = _nn(x, ws[j, part, :])
            if i == 0:
                acc[:, cols] = prod
            elif i < PIECES - 1:
                acc[:, cols] += prod
            else:
                o_ref[:, cols] = (acc[:, cols] + prod).astype(BF)
    last.wait()
    for k in range(XS):
        for z in range(ZS):
            start = pl.multiple_of((z * XS + lax.rem(my_x + k, XS)) * width, width)
            outs[k][:, z * width : (z + 1) * width] = xs[:, pl.ds(start, width)]


def project(x, wq, wk, wv, do):
    t, d = x.shape
    n = wq.shape[1]
    return pl.pallas_call(
        _project_body,
        in_specs=[ANY] * 5,
        out_specs=[VMEM] * (1 + XS),
        out_shape=[jax.ShapeDtypeStruct((t, 4 * n), BF)]
        + [jax.ShapeDtypeStruct((t, d // XS), BF)] * XS,
        scratch_shapes=[
            pltpu.VMEM((t, d), BF),
            pltpu.VMEM((3, d, n), BF),
            pltpu.VMEM((t, 3 * n), F32),
            pltpu.SemaphoreType.DMA((PIECES + 1, 4)),
        ],
        compiler_params=_params(LARGE),
        cost_estimate=_cost(6 * t * d * n, 2 * (t * d + 3 * d * n)),
        name="project",
    )(x, wq, wk, wv, do)


def _stack_body(*refs):
    o_ref = refs[-1]
    for i, r in enumerate(refs[:-1]):
        o_ref[i] = r[...]


def stack(parts, flops):
    shape = (len(parts), *parts[0].shape)
    return pl.pallas_call(
        _stack_body,
        in_specs=[VMEM] * len(parts),
        out_specs=VMEM,
        out_shape=jax.ShapeDtypeStruct(shape, BF),
        compiler_params=_params(SMALL),
        cost_estimate=_cost(flops, 0),
        name="stack",
    )(*parts)


def _pick_kv_body(p1_ref, p2_ref, all_ref, *rest):
    kv_ref = rest[-1]
    n = all_ref.shape[2] // 4

    def one(d, carry):
        for slot, p_ref in enumerate((p1_ref, p2_ref)):
            kv_ref[d, slot] = all_ref[p_ref[d], :, n : 3 * n]
        return carry

    lax.fori_loop(0, all_ref.shape[0], one, 0)


def _pick_qdo_body(p1_ref, p2_ref, all_ref, *rest):
    qdo_ref = rest[-1]
    n = all_ref.shape[2] // 4

    def one(d, carry):
        for slot, p_ref in enumerate((p1_ref, p2_ref)):
            p = p_ref[d]
            qdo_ref[p, slot, :, :n] = all_ref[d, :, :n]
            qdo_ref[p, slot, :, n:] = all_ref[d, :, 3 * n :]
        return carry

    lax.fori_loop(0, all_ref.shape[0], one, 0)


def pick(body, p1, p2, blocks, after):
    docs, rows, n = blocks.shape
    n = n // 4
    return pl.pallas_call(
        body,
        in_specs=[SMEM, SMEM, VMEM] + [VMEM] * len(after),
        out_specs=VMEM,
        out_shape=jax.ShapeDtypeStruct((docs, 2, rows, 2 * n), BF),
        compiler_params=_params(SMALL),
        cost_estimate=_cost(0, 2 * docs * rows * n * 8),
        name="pick",
    )(p1, p2, blocks, *after)


def _attend_body(factor, qkv_ref, kv_ref, *rest):
    gq_ref, st_ref = rest[-2:]
    t, n = gq_ref.shape
    st_ref[...] = jnp.zeros_like(st_ref)
    for h in range(n // HD):
        c = slice(h * HD, (h + 1) * HD)
        q = qkv_ref[:, c]
        k = qkv_ref[:, n + h * HD : n + (h + 1) * HD]
        v = qkv_ref[:, 2 * n + h * HD : 2 * n + (h + 1) * HD]
        do = qkv_ref[:, 3 * n + h * HD : 3 * n + (h + 1) * HD]
        keys, values = [k], [v]
        for s in range(2):
            keys.append(kv_ref[:, s, :, c].reshape(t, HD))
            values.append(kv_ref[:, s, :, n + h * HD : n + (h + 1) * HD].reshape(t, HD))
        sc = [_nt(kk, q) * factor for kk in keys]
        key_at = lax.broadcasted_iota(jnp.int32, (t, t), 0)
        query_at = lax.broadcasted_iota(jnp.int32, (t, t), 1)
        sc[0] = jnp.where(key_at <= query_at, sc[0], -jnp.inf)
        m = functools.reduce(jnp.maximum, [jnp.max(x, axis=0, keepdims=True) for x in sc])
        e = [jnp.exp(x - m) for x in sc]
        il = 1.0 / sum(jnp.sum(x, axis=0, keepdims=True) for x in e)
        p = [x * il for x in e]
        low = [x.astype(BF) for x in p]
        dp = [_nt(vv, do) for vv in values]
        delta = sum(
            jnp.sum(a.astype(F32) * b, axis=0, keepdims=True) for a, b in zip(low, dp)
        )
        ds = [(a * (b - delta)).astype(BF) for a, b in zip(p, dp)]
        gq = sum(_tn(a, kk) for a, kk in zip(ds, keys)) * factor
        gq_ref[:, c] = gq.astype(BF)
        st_ref[3 * h : 3 * h + 1, :] = m
        st_ref[3 * h + 1 : 3 * h + 2, :] = il
        st_ref[3 * h + 2 : 3 * h + 3, :] = delta


def attend(factor, qkv, kv, after):
    t, n = qkv.shape
    n = n // 4
    return pl.pallas_call(
        functools.partial(_attend_body, factor),
        in_specs=[VMEM] * 2 + [ANY] * len(after),
        out_specs=[VMEM] * 2,
        out_shape=[
            jax.ShapeDtypeStruct((t, n), BF),
            jax.ShapeDtypeStruct((8, t), F32),
        ],
        compiler_params=_params(SMALL),
        cost_estimate=_cost(2 * 11 * t * t * n, 4 * t * n * 10, 3 * t * t * n // HD),
        name="attend",
    )(qkv, kv, *after)


def _settle_body(factor, p1_ref, p2_ref, qkv_ref, qdo_ref, *rest):
    gk_ref, gv_ref, both_ref = rest[-3:]
    st_refs = rest[:ZS]
    t, n = gk_ref.shape
    me = lax.axis_index("doc")
    names = [
        sum(jnp.where(p[d] == me, d, 0) for d in range(p1_ref.shape[0]))
        for p in (p1_ref, p2_ref)
    ]
    steps_z = [lax.rem(me // XS - d // XS + ZS, ZS) for d in names]
    steps_x = [lax.rem(lax.rem(me, XS) - lax.rem(d, XS) + XS, XS) for d in names]
    for h in range(n // HD):
        c = slice(h * HD, (h + 1) * HD)
        k = qkv_ref[:, n + h * HD : n + (h + 1) * HD]
        v = qkv_ref[:, 2 * n + h * HD : 2 * n + (h + 1) * HD]
        dk = dv = 0.0
        for s in range(3):
            if s == 2:
                st = st_refs[0][0]
                q, do = qkv_ref[:, c], qkv_ref[:, 3 * n + h * HD : 3 * n + (h + 1) * HD]
            else:
                st = st_refs[0][steps_x[s]]
                for j in range(1, ZS):
                    st = jnp.where(steps_z[s] == j, st_refs[j][steps_x[s]], st)
                q = qdo_ref[:, s, :, c].reshape(t, HD)
                do = qdo_ref[:, s, :, n + h * HD : n + (h + 1) * HD].reshape(t, HD)
            m, il, delta = (st[3 * h + i : 3 * h + i + 1, :] for i in range(3))
            sc = _nt(k, q) * factor
            if s == 2:
                key_at = lax.broadcasted_iota(jnp.int32, (t, t), 0)
                query_at = lax.broadcasted_iota(jnp.int32, (t, t), 1)
                sc = jnp.where(key_at <= query_at, sc, -jnp.inf)
            p = jnp.exp(sc - m) * il
            dp = _nt(v, do)
            ds = (p * (dp - delta)).astype(BF)
            dk = dk + _nn(ds, q) * factor
            dv = dv + _nn(p.astype(BF), do)
        gk, gv = dk.astype(BF), dv.astype(BF)
        gk_ref[:, c] = gk
        gv_ref[:, c] = gv
        both_ref[:, c] = gk
        both_ref[:, n + h * HD : n + (h + 1) * HD] = gv


def settle(factor, p1, p2, qkv, qdo, stats, after):
    t, n = qkv.shape
    n = n // 4
    return pl.pallas_call(
        functools.partial(_settle_body, factor),
        in_specs=[SMEM] * 2 + [VMEM] * (2 + ZS + len(after)),
        out_specs=[VMEM] * 3,
        out_shape=[
            jax.ShapeDtypeStruct((t, n), BF),
            jax.ShapeDtypeStruct((t, n), BF),
            jax.ShapeDtypeStruct((t, 2 * n), BF),
        ],
        compiler_params=_params(SMALL),
        cost_estimate=_cost(2 * 12 * t * t * n, 4 * t * n * 8, 3 * t * t * n // HD),
        name="settle",
    )(p1, p2, qkv, qdo, *stats, *after)


def _wgrad_body(near_ref, far_ref, *refs):
    gq, gkv = refs[0:XS], refs[XS : 2 * XS]
    xs = (near_ref.at[0], near_ref.at[1], far_ref.at[0], near_ref.at[2])
    keep_ref, send_ref = refs[-2:]
    first = lax.axis_index("cuts") == 0
    half, n = keep_ref.shape[1], gq[0].shape[1]
    for z in range(ZS):
        for cols, gs in ((slice(0, n), gq), (slice(n, 3 * n), gkv)):
            acc = None
            for x, g in zip(xs, gs):
                part = _tn(x[:, z * 2 * half : (z + 1) * 2 * half], g[...])
                acc = part if acc is None else acc + part
            top, low = acc[:half], acc[half:]
            keep_ref[z, :, cols] = jnp.where(first, top, low)
            send_ref[z, :, cols] = jnp.where(first, low, top).astype(BF)


def wgrad(near, far, gq, gkv):
    _, t, rows = near.shape
    n = gq[0].shape[1]
    shape = (ZS, rows // (2 * ZS), 3 * n)
    return pl.pallas_call(
        _wgrad_body,
        in_specs=[VMEM] * (2 + 2 * XS),
        out_specs=[VMEM, VMEM],
        out_shape=[jax.ShapeDtypeStruct(shape, F32), jax.ShapeDtypeStruct(shape, BF)],
        compiler_params=_params(SMALL),
        cost_estimate=_cost(2 * XS * t * rows * 3 * n, 2 * XS * t * (rows + 3 * n) + 6 * rows * n),
        name="wgrad",
    )(near, far, *gq, *gkv)


def _xgrad_body(wq_ref, wk_ref, wv_ref, gq_ref, gkv_ref, *rest):
    o_ref = rest[-1]
    n = gq_ref.shape[1]
    block = o_ref.shape[2]
    rb = 256
    for y in range(YS):
        for half in range(2):
            for r in range(block // rb):
                at = (half * YS + y) * block + r * rb
                rows = slice(at, at + rb)
                acc = (
                    _nt(wq_ref[rows], gq_ref[...])
                    + _nt(wk_ref[rows], gkv_ref[:, :n])
                    + _nt(wv_ref[rows], gkv_ref[:, n:])
                )
                o_ref[y, half, r * rb : (r + 1) * rb] = acc.astype(BF)


def xgrad(wq, wk, wv, gq, gkv, after):
    d, n = wq.shape
    t = gq.shape[0]
    return pl.pallas_call(
        _xgrad_body,
        in_specs=[VMEM] * (5 + len(after)),
        out_specs=VMEM,
        out_shape=jax.ShapeDtypeStruct((YS, 2, d // (2 * YS), t), BF),
        compiler_params=_params(SMALL),
        cost_estimate=_cost(6 * t * d * n, 6 * d * n + 8 * t * n + 2 * d * t),
        name="xgrad",
    )(wq, wk, wv, gq, gkv, *after)


def shift_x(v, k):
    pairs = [(z * XS + x, z * XS + (x + k) % XS) for z in range(ZS) for x in range(XS)]
    return lax.ppermute(v, "doc", pairs)


def shift_z(v, k):
    pairs = [(z * XS + x, ((z + k) % ZS) * XS + x) for z in range(ZS) for x in range(XS)]
    return lax.ppermute(v, "doc", pairs)


def shift_y(v, k):
    pairs = [(a * YS + y, a * YS + (y + k) % YS) for a in range(2) for y in range(YS)]
    return lax.ppermute(v, "head", pairs)


def swap_halves(v):
    pairs = [(a * YS + y, (1 - a) * YS + y) for a in range(2) for y in range(YS)]
    return lax.ppermute(v, "head", pairs)


def swap_cores(v):
    return lax.ppermute(v, "cuts", [(0, 1), (1, 0)])


ORDER = (1, 3, 2)


def per_device(
    inputs, weight_query, weight_key, weight_value, grad_output, partner_one, partner_two
):
    x = inputs[0, 0]
    do = grad_output[0, 0]
    t, d = x.shape
    n = weight_query.shape[1]
    factor = 1.0 / math.sqrt(HD)
    docs = lax.axis_size("doc")
    rows = t // docs
    p1, p2 = partner_one[0], partner_two[0]
    me = lax.axis_index("doc")
    my_z = me // XS
    def spread(v):
        return lax.all_to_all(v, "doc", split_axis=0, concat_axis=0, tiled=True)

    qkvd, *cuts = project(x, weight_query, weight_key, weight_value, do)
    blocks = spread(qkvd.reshape(docs, rows, 4 * n))

    near = stack([cuts[0], shift_x(cuts[1], 1), shift_x(cuts[3], 3)], HINT)
    far = stack([shift_x(cuts[2], 2)], HINT)

    kv = spread(pick(_pick_kv_body, p1, p2, blocks, [near]))
    qdo = spread(pick(_pick_qdo_body, p1, p2, blocks, [far]))
    gq, stats = attend(factor, qkvd, kv, [])
    weights = [weight_query, weight_key, weight_value]
    row = jnp.stack([shift_x(stats, k) if k else stats for k in range(XS)])
    all_stats = [shift_z(row, k) if k else row for k in range(ZS)]
    gq_x = {0: gq, **{k: shift_x(gq, k) for k in ORDER}}
    gk, gv, gkv = settle(factor, p1, p2, qkvd, qdo, all_stats, weights)
    gkv_x = {0: gkv, **{k: shift_x(gkv, k) for k in ORDER}}

    terms = xgrad(*weights, gq, gkv, [gq_x[k] for k in ORDER])
    groups = [[a * YS + y for y in range(YS)] for a in range(2)]
    terms = lax.all_to_all(
        terms, "head", split_axis=0, concat_axis=0, tiled=True, axis_index_groups=groups
    )
    mine, theirs = wgrad(
        near,
        far,
        [gq_x[k] for k in range(XS)],
        [gkv_x[k] for k in range(XS)],
    )
    pair = (mine + swap_cores(theirs).astype(F32)).astype(BF)
    total = lax.dynamic_index_in_dim(pair, my_z, axis=0, keepdims=False).astype(F32)
    for k in range(1, ZS):
        out = lax.dynamic_index_in_dim(pair, (my_z + k) % ZS, axis=0, keepdims=False)
        total = total + shift_z(out, k).astype(F32)
    sums = jnp.sum(terms.astype(F32), axis=0)
    my_half = lax.axis_index("head") // YS
    keep = lax.dynamic_index_in_dim(sums, my_half, axis=0, keepdims=False)
    send = lax.dynamic_index_in_dim(sums, 1 - my_half, axis=0, keepdims=False)
    features = (keep + swap_halves(send.astype(BF)).astype(F32)).astype(BF)
    return (
        gk.reshape(1, 1, t, n),
        gv.reshape(1, 1, t, n),
        total[:, :n],
        total[:, n : 2 * n],
        total[:, 2 * n :],
        features.reshape(1, 1, features.shape[0], t),
    )


def solution(mesh):
    in_specs = (
        P("cuts", "doc", None, None),
        P(None, "head"),
        P(None, "head"),
        P(None, "head"),
        P("cuts", "doc", None, "head"),
        P("cuts", None),
        P("cuts", None),
    )
    out_specs = (
        P("cuts", "doc", None, "head"),
        P("cuts", "doc", None, "head"),
        P(("doc", "cuts"), "head"),
        P(("doc", "cuts"), "head"),
        P(("doc", "cuts"), "head"),
        P("cuts", "doc", "head", None),
    )
    return jax.shard_map(
        per_device, mesh=mesh, in_specs=in_specs, out_specs=out_specs, check_vma=False
    )
```

```python
import functools
import math

import jax
import jax.numpy as jnp
from jax import lax
from jax.experimental import pallas as pl
from jax.experimental.pallas import tpu as pltpu
from jax.sharding import PartitionSpec as P

HD = 128
XS = 4
ZS = 4
YS = 4
BF = jnp.bfloat16
F32 = jnp.float32
SMALL = 16 * 1024 * 1024
LARGE = 52 * 1024 * 1024
VMEM = pl.BlockSpec(memory_space=pltpu.VMEM)
SMEM = pl.BlockSpec(memory_space=pltpu.SMEM)
ANY = pl.BlockSpec(memory_space=pl.ANY)


def _params(limit):
    return pltpu.CompilerParams(vmem_limit_bytes=limit)


def _cost(flops, nbytes, trans=0):
    return pl.CostEstimate(flops=flops, bytes_accessed=nbytes, transcendentals=trans)


def _nt(a, b):
    return lax.dot_general(a, b, (((1,), (1,)), ((), ())), preferred_element_type=F32)


def _nn(a, b):
    return lax.dot_general(a, b, (((1,), (0,)), ((), ())), preferred_element_type=F32)


def _tn(a, b):
    return lax.dot_general(a, b, (((0,), (0,)), ((), ())), preferred_element_type=F32)


PIECES = 8
HINT = 30_000_000_000


def _project_body(x_ref, wq_ref, wk_ref, wv_ref, do_ref, o_ref, *rest):
    outs, (xs, ws, acc, sems) = rest[:XS], rest[XS:]
    d, n = wq_ref.shape
    my_x = lax.rem(lax.axis_index("doc"), XS)
    width = d // (ZS * XS)
    kb = d // PIECES
    last = pltpu.make_async_copy(do_ref, o_ref.at[:, 3 * n :], sems.at[PIECES, 0])
    copies = []
    for i in range(PIECES):
        part = slice(i * kb, (i + 1) * kb)
        row = [pltpu.make_async_copy(x_ref.at[:, part], xs.at[:, part], sems.at[i, 0])]
        for j, w in enumerate((wq_ref, wk_ref, wv_ref)):
            row.append(pltpu.make_async_copy(w.at[part, :], ws.at[j, part, :], sems.at[i, j + 1]))
        for c in row:
            c.start()
        copies.append(row)
    last.start()
    for i in range(PIECES):
        part = slice(i * kb, (i + 1) * kb)
        for c in copies[i]:
            c.wait()
        x = xs[:, part]
        for j in range(3):
            cols = slice(j * n, (j + 1) * n)
            prod = _nn(x, ws[j, part, :])
            if i == 0:
                acc[:, cols] = prod
            elif i < PIECES - 1:
                acc[:, cols] += prod
            else:
                o_ref[:, cols] = (acc[:, cols] + prod).astype(BF)
    last.wait()
    quarter = xs.shape[0] // YS
    mine = pl.multiple_of(lax.rem(lax.axis_index("head"), YS) * quarter, quarter)
    for k in range(XS):
        rows = slice(None) if k == 0 else pl.ds(mine, quarter)
        for z in range(ZS):
            start = pl.multiple_of((z * XS + lax.rem(my_x + k, XS)) * width, width)
            outs[k][:, z * width : (z + 1) * width] = xs[rows, pl.ds(start, width)]


def project(x, wq, wk, wv, do):
    t, d = x.shape
    n = wq.shape[1]
    return pl.pallas_call(
        _project_body,
        in_specs=[ANY] * 5,
        out_specs=[VMEM] * (1 + XS),
        out_shape=[jax.ShapeDtypeStruct((t, 4 * n), BF)]
        + [jax.ShapeDtypeStruct((t if k == 0 else t // YS, d // XS), BF) for k in range(XS)],
        scratch_shapes=[
            pltpu.VMEM((t, d), BF),
            pltpu.VMEM((3, d, n), BF),
            pltpu.VMEM((t, 3 * n), F32),
            pltpu.SemaphoreType.DMA((PIECES + 1, 4)),
        ],
        compiler_params=_params(LARGE),
        cost_estimate=_cost(6 * t * d * n, 2 * (t * d + 3 * d * n)),
        name="project",
    )(x, wq, wk, wv, do)


def _stack_body(*refs):
    o_ref = refs[-1]
    for i, r in enumerate(refs[:-1]):
        o_ref[i] = r[...]


def stack(parts):
    shape = (len(parts), *parts[0].shape)
    return pl.pallas_call(
        _stack_body,
        in_specs=[VMEM] * len(parts),
        out_specs=VMEM,
        out_shape=jax.ShapeDtypeStruct(shape, BF),
        compiler_params=_params(SMALL),
        cost_estimate=_cost(HINT, 0),
        name="stack",
    )(*parts)


def _merge_body(own_ref, *refs):
    parts, o_ref = refs[:YS], refs[-1]
    quarter = parts[0].shape[1]
    my_y = lax.rem(lax.axis_index("head"), YS)
    o_ref[0] = own_ref[...]
    for j in range(YS):
        at = pl.multiple_of(lax.rem(my_y + YS - j, YS) * quarter, quarter)
        for k in range(1, XS):
            o_ref[k, pl.ds(at, quarter), :] = parts[j][k - 1]


def merge(own, parts):
    return pl.pallas_call(
        _merge_body,
        in_specs=[VMEM] * (1 + YS),
        out_specs=VMEM,
        out_shape=jax.ShapeDtypeStruct((XS, *own.shape), BF),
        compiler_params=_params(SMALL),
        cost_estimate=_cost(HINT, 0),
        name="merge",
    )(own, *parts)


def _pick_kv_body(p1_ref, p2_ref, all_ref, *rest):
    kv_ref = rest[-1]
    n = all_ref.shape[2] // 4

    def one(d, carry):
        for slot, p_ref in enumerate((p1_ref, p2_ref)):
            kv_ref[d, slot] = all_ref[p_ref[d], :, n : 3 * n]
        return carry

    lax.fori_loop(0, all_ref.shape[0], one, 0)


def _pick_qdo_body(p1_ref, p2_ref, all_ref, *rest):
    qdo_ref = rest[-1]
    n = all_ref.shape[2] // 4

    def one(d, carry):
        for slot, p_ref in enumerate((p1_ref, p2_ref)):
            p = p_ref[d]
            qdo_ref[p, slot, :, :n] = all_ref[d, :, :n]
            qdo_ref[p, slot, :, n:] = all_ref[d, :, 3 * n :]
        return carry

    lax.fori_loop(0, all_ref.shape[0], one, 0)


def pick(body, p1, p2, blocks, after):
    docs, rows, n = blocks.shape
    n = n // 4
    return pl.pallas_call(
        body,
        in_specs=[SMEM, SMEM, VMEM] + [VMEM] * len(after),
        out_specs=VMEM,
        out_shape=jax.ShapeDtypeStruct((docs, 2, rows, 2 * n), BF),
        compiler_params=_params(SMALL),
        cost_estimate=_cost(0, 2 * docs * rows * n * 8),
        name="pick",
    )(p1, p2, blocks, *after)


def _attend_body(factor, qkv_ref, kv_ref, *rest):
    gq_ref, st_ref = rest[-2:]
    t, n = gq_ref.shape
    st_ref[...] = jnp.zeros_like(st_ref)
    for h in range(n // HD):
        c = slice(h * HD, (h + 1) * HD)
        q = qkv_ref[:, c]
        k = qkv_ref[:, n + h * HD : n + (h + 1) * HD]
        v = qkv_ref[:, 2 * n + h * HD : 2 * n + (h + 1) * HD]
        do = qkv_ref[:, 3 * n + h * HD : 3 * n + (h + 1) * HD]
        keys, values = [k], [v]
        for s in range(2):
            keys.append(kv_ref[:, s, :, c].reshape(t, HD))
            values.append(kv_ref[:, s, :, n + h * HD : n + (h + 1) * HD].reshape(t, HD))
        sc = [_nt(kk, q) * factor for kk in keys]
        key_at = lax.broadcasted_iota(jnp.int32, (t, t), 0)
        query_at = lax.broadcasted_iota(jnp.int32, (t, t), 1)
        sc[0] = jnp.where(key_at <= query_at, sc[0], -jnp.inf)
        m = functools.reduce(jnp.maximum, [jnp.max(x, axis=0, keepdims=True) for x in sc])
        e = [jnp.exp(x - m) for x in sc]
        il = 1.0 / sum(jnp.sum(x, axis=0, keepdims=True) for x in e)
        p = [x * il for x in e]
        low = [x.astype(BF) for x in p]
        dp = [_nt(vv, do) for vv in values]
        delta = sum(
            jnp.sum(a.astype(F32) * b, axis=0, keepdims=True) for a, b in zip(low, dp)
        )
        ds = [(a * (b - delta)).astype(BF) for a, b in zip(p, dp)]
        gq = sum(_tn(a, kk) for a, kk in zip(ds, keys)) * factor
        gq_ref[:, c] = gq.astype(BF)
        st_ref[3 * h : 3 * h + 1, :] = m
        st_ref[3 * h + 1 : 3 * h + 2, :] = il
        st_ref[3 * h + 2 : 3 * h + 3, :] = delta


def attend(factor, qkv, kv, after):
    t, n = qkv.shape
    n = n // 4
    return pl.pallas_call(
        functools.partial(_attend_body, factor),
        in_specs=[VMEM] * 2 + [ANY] * len(after),
        out_specs=[VMEM] * 2,
        out_shape=[
            jax.ShapeDtypeStruct((t, n), BF),
            jax.ShapeDtypeStruct((8, t), F32),
        ],
        compiler_params=_params(SMALL),
        cost_estimate=_cost(2 * 11 * t * t * n, 4 * t * n * 10, 3 * t * t * n // HD),
        name="attend",
    )(qkv, kv, *after)


def _settle_body(factor, p1_ref, p2_ref, qkv_ref, qdo_ref, *rest):
    gk_ref, gv_ref, both_ref = rest[-3:]
    st_refs = rest[:ZS]
    t, n = gk_ref.shape
    me = lax.axis_index("doc")
    names = [
        sum(jnp.where(p[d] == me, d, 0) for d in range(p1_ref.shape[0]))
        for p in (p1_ref, p2_ref)
    ]
    steps_z = [lax.rem(me // XS - d // XS + ZS, ZS) for d in names]
    steps_x = [lax.rem(lax.rem(me, XS) - lax.rem(d, XS) + XS, XS) for d in names]
    for h in range(n // HD):
        c = slice(h * HD, (h + 1) * HD)
        k = qkv_ref[:, n + h * HD : n + (h + 1) * HD]
        v = qkv_ref[:, 2 * n + h * HD : 2 * n + (h + 1) * HD]
        dk = dv = 0.0
        for s in range(3):
            if s == 2:
                st = st_refs[0][0]
                q, do = qkv_ref[:, c], qkv_ref[:, 3 * n + h * HD : 3 * n + (h + 1) * HD]
            else:
                st = st_refs[0][steps_x[s]]
                for j in range(1, ZS):
                    st = jnp.where(steps_z[s] == j, st_refs[j][steps_x[s]], st)
                q = qdo_ref[:, s, :, c].reshape(t, HD)
                do = qdo_ref[:, s, :, n + h * HD : n + (h + 1) * HD].reshape(t, HD)
            m, il, delta = (st[3 * h + i : 3 * h + i + 1, :] for i in range(3))
            sc = _nt(k, q) * factor
            if s == 2:
                key_at = lax.broadcasted_iota(jnp.int32, (t, t), 0)
                query_at = lax.broadcasted_iota(jnp.int32, (t, t), 1)
                sc = jnp.where(key_at <= query_at, sc, -jnp.inf)
            p = jnp.exp(sc - m) * il
            dp = _nt(v, do)
            ds = (p * (dp - delta)).astype(BF)
            dk = dk + _nn(ds, q) * factor
            dv = dv + _nn(p.astype(BF), do)
        gk, gv = dk.astype(BF), dv.astype(BF)
        gk_ref[:, c] = gk
        gv_ref[:, c] = gv
        both_ref[:, c] = gk
        both_ref[:, n + h * HD : n + (h + 1) * HD] = gv


def settle(factor, p1, p2, qkv, qdo, stats, after):
    t, n = qkv.shape
    n = n // 4
    return pl.pallas_call(
        functools.partial(_settle_body, factor),
        in_specs=[SMEM] * 2 + [VMEM] * (2 + ZS + len(after)),
        out_specs=[VMEM] * 3,
        out_shape=[
            jax.ShapeDtypeStruct((t, n), BF),
            jax.ShapeDtypeStruct((t, n), BF),
            jax.ShapeDtypeStruct((t, 2 * n), BF),
        ],
        compiler_params=_params(SMALL),
        cost_estimate=_cost(2 * 12 * t * t * n, 4 * t * n * 8, 3 * t * t * n // HD),
        name="settle",
    )(p1, p2, qkv, qdo, *stats, *after)


def _wgrad_body(x_ref, *refs):
    gq, gkv = refs[0:XS], refs[XS : 2 * XS]
    xs = [x_ref.at[k] for k in range(XS)]
    keep_ref, send_ref = refs[-2:]
    first = lax.axis_index("cuts") == 0
    half, n = keep_ref.shape[1], gq[0].shape[1]
    for z in range(ZS):
        for cols, gs in ((slice(0, n), gq), (slice(n, 3 * n), gkv)):
            acc = None
            for x, g in zip(xs, gs):
                part = _tn(x[:, z * 2 * half : (z + 1) * 2 * half], g[...])
                acc = part if acc is None else acc + part
            top, low = acc[:half], acc[half:]
            keep_ref[z, :, cols] = jnp.where(first, top, low).astype(BF)
            send_ref[z, :, cols] = jnp.where(first, low, top).astype(BF)


def wgrad(xs, gq, gkv):
    _, t, rows = xs.shape
    n = gq[0].shape[1]
    shape = (ZS, rows // (2 * ZS), 3 * n)
    return pl.pallas_call(
        _wgrad_body,
        in_specs=[VMEM] * (1 + 2 * XS),
        out_specs=[VMEM, VMEM],
        out_shape=[jax.ShapeDtypeStruct(shape, BF), jax.ShapeDtypeStruct(shape, BF)],
        compiler_params=_params(SMALL),
        cost_estimate=_cost(2 * XS * t * rows * 3 * n, 2 * XS * t * (rows + 3 * n) + 6 * rows * n),
        name="wgrad",
    )(xs, *gq, *gkv)


def _pair_body(keep_ref, got_ref, own_ref, *outs):
    my_z = lax.axis_index("doc") // XS
    own_ref[...] = keep_ref[my_z].astype(F32) + got_ref[my_z].astype(F32)
    for k, o_ref in enumerate(outs):
        to = lax.rem(my_z + k + 1, ZS)
        o_ref[...] = (keep_ref[to].astype(F32) + got_ref[to].astype(F32)).astype(BF)


def pair(keep, got):
    piece = keep.shape[1:]
    return pl.pallas_call(
        _pair_body,
        in_specs=[VMEM] * 2,
        out_specs=[VMEM] * ZS,
        out_shape=[jax.ShapeDtypeStruct(piece, F32)]
        + [jax.ShapeDtypeStruct(piece, BF)] * (ZS - 1),
        compiler_params=_params(SMALL),
        cost_estimate=_cost(4 * HINT // 30, 6 * keep.size),
        name="pair",
    )(keep, got)


def _xgrad_body(wq_ref, wk_ref, wv_ref, gq_ref, gkv_ref, *rest):
    o_ref = rest[-1]
    n = gq_ref.shape[1]
    block = o_ref.shape[2]
    rb = 256
    for y in range(YS):
        for half in range(2):
            for r in range(block // rb):
                at = (half * YS + y) * block + r * rb
                rows = slice(at, at + rb)
                acc = (
                    _nt(wq_ref[rows], gq_ref[...])
                    + _nt(wk_ref[rows], gkv_ref[:, :n])
                    + _nt(wv_ref[rows], gkv_ref[:, n:])
                )
                o_ref[y, half, r * rb : (r + 1) * rb] = acc.astype(BF)


def xgrad(wq, wk, wv, gq, gkv, after):
    d, n = wq.shape
    t = gq.shape[0]
    return pl.pallas_call(
        _xgrad_body,
        in_specs=[VMEM] * (5 + len(after)),
        out_specs=VMEM,
        out_shape=jax.ShapeDtypeStruct((YS, 2, d // (2 * YS), t), BF),
        compiler_params=_params(SMALL),
        cost_estimate=_cost(6 * t * d * n, 6 * d * n + 8 * t * n + 2 * d * t),
        name="xgrad",
    )(wq, wk, wv, gq, gkv, *after)


def shift_x(v, k):
    pairs = [(z * XS + x, z * XS + (x + k) % XS) for z in range(ZS) for x in range(XS)]
    return lax.ppermute(v, "doc", pairs)


def shift_z(v, k):
    pairs = [(z * XS + x, ((z + k) % ZS) * XS + x) for z in range(ZS) for x in range(XS)]
    return lax.ppermute(v, "doc", pairs)


def shift_y(v, k):
    pairs = [(a * YS + y, a * YS + (y + k) % YS) for a in range(2) for y in range(YS)]
    return lax.ppermute(v, "head", pairs)


def swap_halves(v):
    pairs = [(a * YS + y, (1 - a) * YS + y) for a in range(2) for y in range(YS)]
    return lax.ppermute(v, "head", pairs)


def swap_cores(v):
    return lax.ppermute(v, "cuts", [(0, 1), (1, 0)])


ORDER = (1, 3, 2)


def per_device(
    inputs, weight_query, weight_key, weight_value, grad_output, partner_one, partner_two
):
    x = inputs[0, 0]
    do = grad_output[0, 0]
    t, d = x.shape
    n = weight_query.shape[1]
    factor = 1.0 / math.sqrt(HD)
    docs = lax.axis_size("doc")
    rows = t // docs
    p1, p2 = partner_one[0], partner_two[0]
    def spread(v):
        return lax.all_to_all(v, "doc", split_axis=0, concat_axis=0, tiled=True)

    qkvd, *cuts = project(x, weight_query, weight_key, weight_value, do)
    blocks = spread(qkvd.reshape(docs, rows, 4 * n))

    quarters = stack([shift_x(cuts[k], k) for k in range(1, XS)])
    columns = merge(cuts[0], [shift_y(quarters, j) if j else quarters for j in range(YS)])

    kv = spread(pick(_pick_kv_body, p1, p2, blocks, [quarters]))
    qdo = spread(pick(_pick_qdo_body, p1, p2, blocks, [columns]))
    gq, stats = attend(factor, qkvd, kv, [])
    weights = [weight_query, weight_key, weight_value]
    row = jnp.stack([shift_x(stats, k) if k else stats for k in range(XS)])
    all_stats = [shift_z(row, k) if k else row for k in range(ZS)]
    gq_x = {0: gq, **{k: shift_x(gq, k) for k in ORDER}}
    gk, gv, gkv = settle(factor, p1, p2, qkvd, qdo, all_stats, weights)
    gkv_x = {0: gkv, **{k: shift_x(gkv, k) for k in ORDER}}

    terms = xgrad(*weights, gq, gkv, [gq_x[k] for k in ORDER])
    groups = [[a * YS + y for y in range(YS)] for a in range(2)]
    terms = lax.all_to_all(
        terms, "head", split_axis=0, concat_axis=0, tiled=True, axis_index_groups=groups
    )
    mine, theirs = wgrad(
        columns,
        [gq_x[k] for k in range(XS)],
        [gkv_x[k] for k in range(XS)],
    )
    total, *pieces = pair(mine, swap_cores(theirs))
    for k in range(1, ZS):
        total = total + shift_z(pieces[k - 1], k).astype(F32)
    sums = jnp.sum(terms.astype(F32), axis=0)
    my_half = lax.axis_index("head") // YS
    keep = lax.dynamic_index_in_dim(sums, my_half, axis=0, keepdims=False)
    send = lax.dynamic_index_in_dim(sums, 1 - my_half, axis=0, keepdims=False)
    features = (keep + swap_halves(send.astype(BF)).astype(F32)).astype(BF)
    return (
        gk.reshape(1, 1, t, n),
        gv.reshape(1, 1, t, n),
        total[:, :n],
        total[:, n : 2 * n],
        total[:, 2 * n :],
        features.reshape(1, 1, features.shape[0], t),
    )


def solution(mesh):
    in_specs = (
        P("cuts", "doc", None, None),
        P(None, "head"),
        P(None, "head"),
        P(None, "head"),
        P("cuts", "doc", None, "head"),
        P("cuts", None),
        P("cuts", None),
    )
    out_specs = (
        P("cuts", "doc", None, "head"),
        P("cuts", "doc", None, "head"),
        P(("doc", "cuts"), "head"),
        P(("doc", "cuts"), "head"),
        P(("doc", "cuts"), "head"),
        P("cuts", "doc", "head", None),
    )
    return jax.shard_map(
        per_device, mesh=mesh, in_specs=in_specs, out_specs=out_specs, check_vma=False
    )
```

```python
import functools
import math

import jax
import jax.numpy as jnp
from jax import lax
from jax.experimental import pallas as pl
from jax.experimental.pallas import tpu as pltpu
from jax.sharding import PartitionSpec as P

HD = 128
XS = 4
ZS = 4
YS = 4
BF = jnp.bfloat16
F32 = jnp.float32
SMALL = 16 * 1024 * 1024
LARGE = 52 * 1024 * 1024
VMEM = pl.BlockSpec(memory_space=pltpu.VMEM)
SMEM = pl.BlockSpec(memory_space=pltpu.SMEM)
ANY = pl.BlockSpec(memory_space=pl.ANY)


def _params(limit):
    return pltpu.CompilerParams(vmem_limit_bytes=limit)


def _cost(flops, nbytes, trans=0):
    return pl.CostEstimate(flops=flops, bytes_accessed=nbytes, transcendentals=trans)


def _nt(a, b):
    return lax.dot_general(a, b, (((1,), (1,)), ((), ())), preferred_element_type=F32)


def _nn(a, b):
    return lax.dot_general(a, b, (((1,), (0,)), ((), ())), preferred_element_type=F32)


def _tn(a, b):
    return lax.dot_general(a, b, (((0,), (0,)), ((), ())), preferred_element_type=F32)


PIECES = 8
HINT = 30_000_000_000


def _project_body(x_ref, wq_ref, wk_ref, wv_ref, do_ref, o_ref, *rest):
    outs, (xs, ws, acc, sems) = rest[:XS], rest[XS:]
    d, n = wq_ref.shape
    my_x = lax.rem(lax.axis_index("doc"), XS)
    width = d // (ZS * XS)
    kb = d // PIECES
    last = pltpu.make_async_copy(do_ref, o_ref.at[:, 3 * n :], sems.at[PIECES, 0])
    copies = []
    for i in range(PIECES):
        part = slice(i * kb, (i + 1) * kb)
        row = [pltpu.make_async_copy(x_ref.at[:, part], xs.at[:, part], sems.at[i, 0])]
        for j, w in enumerate((wq_ref, wk_ref, wv_ref)):
            row.append(pltpu.make_async_copy(w.at[part, :], ws.at[j, part, :], sems.at[i, j + 1]))
        for c in row:
            c.start()
        copies.append(row)
    last.start()
    for i in range(PIECES):
        part = slice(i * kb, (i + 1) * kb)
        for c in copies[i]:
            c.wait()
        x = xs[:, part]
        for j in range(3):
            cols = slice(j * n, (j + 1) * n)
            prod = _nn(x, ws[j, part, :])
            if i == 0:
                acc[:, cols] = prod
            elif i < PIECES - 1:
                acc[:, cols] += prod
            else:
                o_ref[:, cols] = (acc[:, cols] + prod).astype(BF)
    last.wait()
    quarter = xs.shape[0] // YS
    mine = pl.multiple_of(lax.rem(lax.axis_index("head"), YS) * quarter, quarter)
    for k in range(XS):
        rows = slice(None) if k == 0 else pl.ds(mine, quarter)
        for z in range(ZS):
            start = pl.multiple_of((z * XS + lax.rem(my_x + k, XS)) * width, width)
            outs[k][:, z * width : (z + 1) * width] = xs[rows, pl.ds(start, width)]


def project(x, wq, wk, wv, do):
    t, d = x.shape
    n = wq.shape[1]
    return pl.pallas_call(
        _project_body,
        in_specs=[ANY] * 5,
        out_specs=[VMEM] * (1 + XS),
        out_shape=[jax.ShapeDtypeStruct((t, 4 * n), BF)]
        + [jax.ShapeDtypeStruct((t if k == 0 else t // YS, d // XS), BF) for k in range(XS)],
        scratch_shapes=[
            pltpu.VMEM((t, d), BF),
            pltpu.VMEM((3, d, n), BF),
            pltpu.VMEM((t, 3 * n), F32),
            pltpu.SemaphoreType.DMA((PIECES + 1, 4)),
        ],
        compiler_params=_params(LARGE),
        cost_estimate=_cost(6 * t * d * n, 2 * (t * d + 3 * d * n)),
        name="project",
    )(x, wq, wk, wv, do)


def _stack_body(*refs):
    o_ref = refs[-1]
    for i, r in enumerate(refs[:-1]):
        o_ref[i] = r[...]


def stack(parts):
    shape = (len(parts), *parts[0].shape)
    return pl.pallas_call(
        _stack_body,
        in_specs=[VMEM] * len(parts),
        out_specs=VMEM,
        out_shape=jax.ShapeDtypeStruct(shape, BF),
        compiler_params=_params(SMALL),
        cost_estimate=_cost(HINT, 0),
        name="stack",
    )(*parts)


def _merge_body(own_ref, *refs):
    parts, o_ref = refs[:YS], refs[-1]
    quarter = parts[0].shape[1]
    my_y = lax.rem(lax.axis_index("head"), YS)
    o_ref[0] = own_ref[...]
    for j in range(YS):
        at = pl.multiple_of(lax.rem(my_y + YS - j, YS) * quarter, quarter)
        for k in range(1, XS):
            o_ref[k, pl.ds(at, quarter), :] = parts[j][k - 1]


def merge(own, parts):
    return pl.pallas_call(
        _merge_body,
        in_specs=[VMEM] * (1 + YS),
        out_specs=VMEM,
        out_shape=jax.ShapeDtypeStruct((XS, *own.shape), BF),
        compiler_params=_params(SMALL),
        cost_estimate=_cost(HINT, 0),
        name="merge",
    )(own, *parts)


def _pick_kv_body(p1_ref, p2_ref, all_ref, *rest):
    kv_ref = rest[-1]
    n = all_ref.shape[2] // 4

    def one(d, carry):
        for slot, p_ref in enumerate((p1_ref, p2_ref)):
            kv_ref[d, slot] = all_ref[p_ref[d], :, n : 3 * n]
        return carry

    lax.fori_loop(0, all_ref.shape[0], one, 0)


def _pick_qdo_body(p1_ref, p2_ref, all_ref, *rest):
    qdo_ref = rest[-1]
    n = all_ref.shape[2] // 4

    def one(d, carry):
        for slot, p_ref in enumerate((p1_ref, p2_ref)):
            p = p_ref[d]
            qdo_ref[p, slot, :, :n] = all_ref[d, :, :n]
            qdo_ref[p, slot, :, n:] = all_ref[d, :, 3 * n :]
        return carry

    lax.fori_loop(0, all_ref.shape[0], one, 0)


def pick(body, p1, p2, blocks, after):
    docs, rows, n = blocks.shape
    n = n // 4
    return pl.pallas_call(
        body,
        in_specs=[SMEM, SMEM, VMEM] + [VMEM] * len(after),
        out_specs=VMEM,
        out_shape=jax.ShapeDtypeStruct((docs, 2, rows, 2 * n), BF),
        compiler_params=_params(SMALL),
        cost_estimate=_cost(0, 2 * docs * rows * n * 8),
        name="pick",
    )(p1, p2, blocks, *after)


def _attend_body(factor, qkv_ref, kv_ref, *rest):
    gq_ref, st_ref = rest[-2:]
    t, n = gq_ref.shape
    st_ref[...] = jnp.zeros_like(st_ref)
    for h in range(n // HD):
        c = slice(h * HD, (h + 1) * HD)
        q = qkv_ref[:, c]
        k = qkv_ref[:, n + h * HD : n + (h + 1) * HD]
        v = qkv_ref[:, 2 * n + h * HD : 2 * n + (h + 1) * HD]
        do = qkv_ref[:, 3 * n + h * HD : 3 * n + (h + 1) * HD]
        keys, values = [k], [v]
        for s in range(2):
            keys.append(kv_ref[:, s, :, c].reshape(t, HD))
            values.append(kv_ref[:, s, :, n + h * HD : n + (h + 1) * HD].reshape(t, HD))
        sc = [_nt(kk, q) * factor for kk in keys]
        key_at = lax.broadcasted_iota(jnp.int32, (t, t), 0)
        query_at = lax.broadcasted_iota(jnp.int32, (t, t), 1)
        sc[0] = jnp.where(key_at <= query_at, sc[0], -jnp.inf)
        m = functools.reduce(jnp.maximum, [jnp.max(x, axis=0, keepdims=True) for x in sc])
        e = [jnp.exp(x - m) for x in sc]
        il = 1.0 / sum(jnp.sum(x, axis=0, keepdims=True) for x in e)
        p = [x * il for x in e]
        low = [x.astype(BF) for x in p]
        dp = [_nt(vv, do) for vv in values]
        delta = sum(
            jnp.sum(a.astype(F32) * b, axis=0, keepdims=True) for a, b in zip(low, dp)
        )
        ds = [(a * (b - delta)).astype(BF) for a, b in zip(p, dp)]
        gq = sum(_tn(a, kk) for a, kk in zip(ds, keys)) * factor
        gq_ref[:, c] = gq.astype(BF)
        st_ref[3 * h : 3 * h + 1, :] = m
        st_ref[3 * h + 1 : 3 * h + 2, :] = il
        st_ref[3 * h + 2 : 3 * h + 3, :] = delta


def attend(factor, qkv, kv, after):
    t, n = qkv.shape
    n = n // 4
    return pl.pallas_call(
        functools.partial(_attend_body, factor),
        in_specs=[VMEM] * 2 + [ANY] * len(after),
        out_specs=[VMEM] * 2,
        out_shape=[
            jax.ShapeDtypeStruct((t, n), BF),
            jax.ShapeDtypeStruct((8, t), F32),
        ],
        compiler_params=_params(SMALL),
        cost_estimate=_cost(2 * 11 * t * t * n, 4 * t * n * 10, 3 * t * t * n // HD),
        name="attend",
    )(qkv, kv, *after)


def _settle_body(factor, p1_ref, p2_ref, qkv_ref, qdo_ref, *rest):
    gk_ref, gv_ref, both_ref = rest[-3:]
    st_refs = rest[:ZS]
    t, n = gk_ref.shape
    me = lax.axis_index("doc")
    names = [
        sum(jnp.where(p[d] == me, d, 0) for d in range(p1_ref.shape[0]))
        for p in (p1_ref, p2_ref)
    ]
    steps_z = [lax.rem(me // XS - d // XS + ZS, ZS) for d in names]
    steps_x = [lax.rem(lax.rem(me, XS) - lax.rem(d, XS) + XS, XS) for d in names]
    for h in range(n // HD):
        c = slice(h * HD, (h + 1) * HD)
        k = qkv_ref[:, n + h * HD : n + (h + 1) * HD]
        v = qkv_ref[:, 2 * n + h * HD : 2 * n + (h + 1) * HD]
        dk = dv = 0.0
        for s in range(3):
            if s == 2:
                st = st_refs[0][0]
                q, do = qkv_ref[:, c], qkv_ref[:, 3 * n + h * HD : 3 * n + (h + 1) * HD]
            else:
                st = st_refs[0][steps_x[s]]
                for j in range(1, ZS):
                    st = jnp.where(steps_z[s] == j, st_refs[j][steps_x[s]], st)
                q = qdo_ref[:, s, :, c].reshape(t, HD)
                do = qdo_ref[:, s, :, n + h * HD : n + (h + 1) * HD].reshape(t, HD)
            m, il, delta = (st[3 * h + i : 3 * h + i + 1, :] for i in range(3))
            sc = _nt(k, q) * factor
            if s == 2:
                key_at = lax.broadcasted_iota(jnp.int32, (t, t), 0)
                query_at = lax.broadcasted_iota(jnp.int32, (t, t), 1)
                sc = jnp.where(key_at <= query_at, sc, -jnp.inf)
            p = jnp.exp(sc - m) * il
            dp = _nt(v, do)
            ds = (p * (dp - delta)).astype(BF)
            dk = dk + _nn(ds, q) * factor
            dv = dv + _nn(p.astype(BF), do)
        gk, gv = dk.astype(BF), dv.astype(BF)
        gk_ref[:, c] = gk
        gv_ref[:, c] = gv
        both_ref[:, c] = gk
        both_ref[:, n + h * HD : n + (h + 1) * HD] = gv


def settle(factor, p1, p2, qkv, qdo, stats, after):
    t, n = qkv.shape
    n = n // 4
    return pl.pallas_call(
        functools.partial(_settle_body, factor),
        in_specs=[SMEM] * 2 + [VMEM] * (2 + ZS + len(after)),
        out_specs=[VMEM] * 3,
        out_shape=[
            jax.ShapeDtypeStruct((t, n), BF),
            jax.ShapeDtypeStruct((t, n), BF),
            jax.ShapeDtypeStruct((t, 2 * n), BF),
        ],
        compiler_params=_params(SMALL),
        cost_estimate=_cost(2 * 12 * t * t * n, 4 * t * n * 8, 3 * t * t * n // HD),
        name="settle",
    )(p1, p2, qkv, qdo, *stats, *after)


def _wgrad_body(flip, x_ref, *refs):
    gq, gkv, o_ref = refs[0:XS], refs[XS : 2 * XS], refs[2 * XS]
    half, n = o_ref.shape[1], gq[0].shape[1]
    core = lax.axis_index("cuts")
    if flip:
        core = 1 - core
    at = pl.multiple_of(core * half, half)
    xs = [
        jnp.concatenate([x_ref[k, :, pl.ds(z * 2 * half + at, half)] for z in range(ZS)], axis=1)
        for k in range(XS)
    ]
    for cols, gs in ((slice(0, n), gq), (slice(n, 2 * n), gkv), (slice(2 * n, 3 * n), gkv)):
        acc = None
        for x, g in zip(xs, gs):
            right = g[...] if gs is gq else g[:, cols.start - n : cols.stop - n]
            part = _tn(x, right)
            acc = part if acc is None else acc + part
        for z in range(ZS):
            o_ref[z, :, cols] = acc[z * half : (z + 1) * half].astype(BF)


def wgrad(flip, xs, gq, gkv):
    _, t, rows = xs.shape
    n = gq[0].shape[1]
    return pl.pallas_call(
        functools.partial(_wgrad_body, flip),
        in_specs=[VMEM] * (1 + 2 * XS),
        out_specs=VMEM,
        out_shape=jax.ShapeDtypeStruct((ZS, rows // (2 * ZS), 3 * n), BF),
        compiler_params=_params(SMALL),
        cost_estimate=_cost(3 * XS * t * rows * 3 * n, 2 * XS * t * (rows + 3 * n) + 3 * rows * n),
        name="wgrad",
    )(xs, *gq, *gkv)


def _pair_body(keep_ref, got_ref, own_ref, *outs):
    my_z = lax.axis_index("doc") // XS
    own_ref[...] = keep_ref[my_z].astype(F32) + got_ref[my_z].astype(F32)
    for k, o_ref in enumerate(outs):
        to = lax.rem(my_z + k + 1, ZS)
        o_ref[...] = (keep_ref[to].astype(F32) + got_ref[to].astype(F32)).astype(BF)


def pair(keep, got):
    piece = keep.shape[1:]
    return pl.pallas_call(
        _pair_body,
        in_specs=[VMEM] * 2,
        out_specs=[VMEM] * ZS,
        out_shape=[jax.ShapeDtypeStruct(piece, F32)]
        + [jax.ShapeDtypeStruct(piece, BF)] * (ZS - 1),
        compiler_params=_params(SMALL),
        cost_estimate=_cost(8 * HINT // 30, 6 * keep.size),
        name="pair",
    )(keep, got)


def _xgrad_body(wq_ref, wk_ref, wv_ref, gq_ref, gkv_ref, *rest):
    o_ref = rest[-1]
    n = gq_ref.shape[1]
    block = o_ref.shape[2]
    rb = 256
    for y in range(YS):
        for half in range(2):
            for r in range(block // rb):
                at = (half * YS + y) * block + r * rb
                rows = slice(at, at + rb)
                acc = (
                    _nt(wq_ref[rows], gq_ref[...])
                    + _nt(wk_ref[rows], gkv_ref[:, :n])
                    + _nt(wv_ref[rows], gkv_ref[:, n:])
                )
                o_ref[y, half, r * rb : (r + 1) * rb] = acc.astype(BF)


def xgrad(wq, wk, wv, gq, gkv, after):
    d, n = wq.shape
    t = gq.shape[0]
    return pl.pallas_call(
        _xgrad_body,
        in_specs=[VMEM] * (5 + len(after)),
        out_specs=VMEM,
        out_shape=jax.ShapeDtypeStruct((YS, 2, d // (2 * YS), t), BF),
        compiler_params=_params(SMALL),
        cost_estimate=_cost(6 * t * d * n, 6 * d * n + 8 * t * n + 2 * d * t),
        name="xgrad",
    )(wq, wk, wv, gq, gkv, *after)


def shift_x(v, k):
    pairs = [(z * XS + x, z * XS + (x + k) % XS) for z in range(ZS) for x in range(XS)]
    return lax.ppermute(v, "doc", pairs)


def shift_z(v, k):
    pairs = [(z * XS + x, ((z + k) % ZS) * XS + x) for z in range(ZS) for x in range(XS)]
    return lax.ppermute(v, "doc", pairs)


def shift_y(v, k):
    pairs = [(a * YS + y, a * YS + (y + k) % YS) for a in range(2) for y in range(YS)]
    return lax.ppermute(v, "head", pairs)


def swap_halves(v):
    pairs = [(a * YS + y, (1 - a) * YS + y) for a in range(2) for y in range(YS)]
    return lax.ppermute(v, "head", pairs)


def swap_cores(v):
    return lax.ppermute(v, "cuts", [(0, 1), (1, 0)])


ORDER = (1, 3, 2)


def per_device(
    inputs, weight_query, weight_key, weight_value, grad_output, partner_one, partner_two
):
    x = inputs[0, 0]
    do = grad_output[0, 0]
    t, d = x.shape
    n = weight_query.shape[1]
    factor = 1.0 / math.sqrt(HD)
    docs = lax.axis_size("doc")
    rows = t // docs
    p1, p2 = partner_one[0], partner_two[0]
    def spread(v):
        return lax.all_to_all(v, "doc", split_axis=0, concat_axis=0, tiled=True)

    qkvd, *cuts = project(x, weight_query, weight_key, weight_value, do)
    blocks = spread(qkvd.reshape(docs, rows, 4 * n))

    quarters = stack([shift_x(cuts[k], k) for k in range(1, XS)])
    columns = merge(cuts[0], [shift_y(quarters, j) if j else quarters for j in range(YS)])

    kv = spread(pick(_pick_kv_body, p1, p2, blocks, [quarters]))
    qdo = spread(pick(_pick_qdo_body, p1, p2, blocks, [columns]))
    gq, stats = attend(factor, qkvd, kv, [])
    weights = [weight_query, weight_key, weight_value]
    row = jnp.stack([shift_x(stats, k) if k else stats for k in range(XS)])
    all_stats = [shift_z(row, k) if k else row for k in range(ZS)]
    gq_x = {0: gq, **{k: shift_x(gq, k) for k in ORDER}}
    gk, gv, gkv = settle(factor, p1, p2, qkvd, qdo, all_stats, weights)
    gkv_x = {0: gkv, **{k: shift_x(gkv, k) for k in ORDER}}

    terms = xgrad(*weights, gq, gkv, [gq_x[k] for k in ORDER])
    groups = [[a * YS + y for y in range(YS)] for a in range(2)]
    terms = lax.all_to_all(
        terms, "head", split_axis=0, concat_axis=0, tiled=True, axis_index_groups=groups
    )
    operands = (columns, [gq_x[k] for k in range(XS)], [gkv_x[k] for k in range(XS)])
    theirs = wgrad(True, *operands)
    mine = wgrad(False, *operands)
    total, *pieces = pair(mine, swap_cores(theirs))
    for k in range(1, ZS):
        total = total + shift_z(pieces[k - 1], k).astype(F32)
    sums = jnp.sum(terms.astype(F32), axis=0)
    my_half = lax.axis_index("head") // YS
    keep = lax.dynamic_index_in_dim(sums, my_half, axis=0, keepdims=False)
    send = lax.dynamic_index_in_dim(sums, 1 - my_half, axis=0, keepdims=False)
    features = (keep + swap_halves(send.astype(BF)).astype(F32)).astype(BF)
    return (
        gk.reshape(1, 1, t, n),
        gv.reshape(1, 1, t, n),
        total[:, :n],
        total[:, n : 2 * n],
        total[:, 2 * n :],
        features.reshape(1, 1, features.shape[0], t),
    )


def solution(mesh):
    in_specs = (
        P("cuts", "doc", None, None),
        P(None, "head"),
        P(None, "head"),
        P(None, "head"),
        P("cuts", "doc", None, "head"),
        P("cuts", None),
        P("cuts", None),
    )
    out_specs = (
        P("cuts", "doc", None, "head"),
        P("cuts", "doc", None, "head"),
        P(("doc", "cuts"), "head"),
        P(("doc", "cuts"), "head"),
        P(("doc", "cuts"), "head"),
        P("cuts", "doc", "head", None),
    )
    return jax.shard_map(
        per_device, mesh=mesh, in_specs=in_specs, out_specs=out_specs, check_vma=False
    )
```

```python
import functools
import math

import jax
import jax.numpy as jnp
from jax import lax
from jax.experimental import pallas as pl
from jax.experimental.pallas import tpu as pltpu
from jax.sharding import PartitionSpec as P

HD = 128
XS = 4
ZS = 4
YS = 4
BF = jnp.bfloat16
F32 = jnp.float32
SMALL = 16 * 1024 * 1024
LARGE = 52 * 1024 * 1024
VMEM = pl.BlockSpec(memory_space=pltpu.VMEM)
SMEM = pl.BlockSpec(memory_space=pltpu.SMEM)
ANY = pl.BlockSpec(memory_space=pl.ANY)
HBM = pl.BlockSpec(memory_space=pltpu.HBM)


def _params(limit):
    return pltpu.CompilerParams(vmem_limit_bytes=limit)


def _cost(flops, nbytes, trans=0):
    return pl.CostEstimate(flops=flops, bytes_accessed=nbytes, transcendentals=trans)


def _nt(a, b):
    return lax.dot_general(a, b, (((1,), (1,)), ((), ())), preferred_element_type=F32)


def _nn(a, b):
    return lax.dot_general(a, b, (((1,), (0,)), ((), ())), preferred_element_type=F32)


def _tn(a, b):
    return lax.dot_general(a, b, (((0,), (0,)), ((), ())), preferred_element_type=F32)


PIECES = 8
HINT = 30_000_000_000


def _project_body(x_ref, wq_ref, wk_ref, wv_ref, do_ref, o_ref, *rest):
    outs, (xs, ws, acc, sems) = rest[:XS], rest[XS:]
    d, n = wq_ref.shape
    my_x = lax.rem(lax.axis_index("doc"), XS)
    width = d // (ZS * XS)
    kb = d // PIECES
    last = pltpu.make_async_copy(do_ref, o_ref.at[:, 3 * n :], sems.at[PIECES, 0])
    copies = []
    for i in range(PIECES):
        part = slice(i * kb, (i + 1) * kb)
        row = [pltpu.make_async_copy(x_ref.at[:, part], xs.at[:, part], sems.at[i, 0])]
        for j, w in enumerate((wq_ref, wk_ref, wv_ref)):
            row.append(pltpu.make_async_copy(w.at[part, :], ws.at[j, part, :], sems.at[i, j + 1]))
        for c in row:
            c.start()
        copies.append(row)
    last.start()
    for i in range(PIECES):
        part = slice(i * kb, (i + 1) * kb)
        for c in copies[i]:
            c.wait()
        x = xs[:, part]
        for j in range(3):
            cols = slice(j * n, (j + 1) * n)
            prod = _nn(x, ws[j, part, :])
            if i == 0:
                acc[:, cols] = prod
            elif i < PIECES - 1:
                acc[:, cols] += prod
            else:
                o_ref[:, cols] = (acc[:, cols] + prod).astype(BF)
    last.wait()
    quarter = xs.shape[0] // YS
    mine = pl.multiple_of(lax.rem(lax.axis_index("head"), YS) * quarter, quarter)
    for k in range(XS):
        rows = slice(None) if k == 0 else pl.ds(mine, quarter)
        for z in range(ZS):
            start = pl.multiple_of((z * XS + lax.rem(my_x + k, XS)) * width, width)
            outs[k][:, z * width : (z + 1) * width] = xs[rows, pl.ds(start, width)]


def project(x, wq, wk, wv, do):
    t, d = x.shape
    n = wq.shape[1]
    return pl.pallas_call(
        _project_body,
        in_specs=[ANY] * 5,
        out_specs=[VMEM] * (1 + XS),
        out_shape=[jax.ShapeDtypeStruct((t, 4 * n), BF)]
        + [jax.ShapeDtypeStruct((t if k == 0 else t // YS, d // XS), BF) for k in range(XS)],
        scratch_shapes=[
            pltpu.VMEM((t, d), BF),
            pltpu.VMEM((3, d, n), BF),
            pltpu.VMEM((t, 3 * n), F32),
            pltpu.SemaphoreType.DMA((PIECES + 1, 4)),
        ],
        compiler_params=_params(LARGE),
        cost_estimate=_cost(6 * t * d * n, 2 * (t * d + 3 * d * n)),
        name="project",
    )(x, wq, wk, wv, do)


def _stack_body(*refs):
    o_ref = refs[-1]
    for i, r in enumerate(refs[:-1]):
        o_ref[i] = r[...]


def stack(parts):
    shape = (len(parts), *parts[0].shape)
    return pl.pallas_call(
        _stack_body,
        in_specs=[VMEM] * len(parts),
        out_specs=VMEM,
        out_shape=jax.ShapeDtypeStruct(shape, BF),
        compiler_params=_params(SMALL),
        cost_estimate=_cost(HINT, 0),
        name="stack",
    )(*parts)


def _merge_body(own_ref, *refs):
    parts, o_ref = refs[:YS], refs[-1]
    quarter = parts[0].shape[1]
    my_y = lax.rem(lax.axis_index("head"), YS)
    o_ref[0] = own_ref[...]
    for j in range(YS):
        at = pl.multiple_of(lax.rem(my_y + YS - j, YS) * quarter, quarter)
        for k in range(1, XS):
            o_ref[k, pl.ds(at, quarter), :] = parts[j][k - 1]


def merge(own, parts):
    return pl.pallas_call(
        _merge_body,
        in_specs=[VMEM] * (1 + YS),
        out_specs=VMEM,
        out_shape=jax.ShapeDtypeStruct((XS, *own.shape), BF),
        compiler_params=_params(SMALL),
        cost_estimate=_cost(HINT, 0),
        name="merge",
    )(own, *parts)


def _pick_kv_body(p1_ref, p2_ref, all_ref, *rest):
    kv_ref = rest[-1]
    n = all_ref.shape[2] // 4

    def one(d, carry):
        for slot, p_ref in enumerate((p1_ref, p2_ref)):
            kv_ref[d, slot] = all_ref[p_ref[d], :, n : 3 * n]
        return carry

    lax.fori_loop(0, all_ref.shape[0], one, 0)


def _pick_qdo_body(p1_ref, p2_ref, all_ref, *rest):
    qdo_ref = rest[-1]
    n = all_ref.shape[2] // 4

    def one(d, carry):
        for slot, p_ref in enumerate((p1_ref, p2_ref)):
            p = p_ref[d]
            qdo_ref[p, slot, :, :n] = all_ref[d, :, :n]
            qdo_ref[p, slot, :, n:] = all_ref[d, :, 3 * n :]
        return carry

    lax.fori_loop(0, all_ref.shape[0], one, 0)


def pick(body, p1, p2, blocks, after):
    docs, rows, n = blocks.shape
    n = n // 4
    return pl.pallas_call(
        body,
        in_specs=[SMEM, SMEM, VMEM] + [VMEM] * len(after),
        out_specs=VMEM,
        out_shape=jax.ShapeDtypeStruct((docs, 2, rows, 2 * n), BF),
        compiler_params=_params(SMALL),
        cost_estimate=_cost(0, 2 * docs * rows * n * 8),
        name="pick",
    )(p1, p2, blocks, *after)


def _attend_body(factor, qkv_ref, kv_ref, *rest):
    gq_ref, st_ref = rest[-2:]
    t, n = gq_ref.shape
    st_ref[...] = jnp.zeros_like(st_ref)
    for h in range(n // HD):
        c = slice(h * HD, (h + 1) * HD)
        q = qkv_ref[:, c]
        k = qkv_ref[:, n + h * HD : n + (h + 1) * HD]
        v = qkv_ref[:, 2 * n + h * HD : 2 * n + (h + 1) * HD]
        do = qkv_ref[:, 3 * n + h * HD : 3 * n + (h + 1) * HD]
        keys, values = [k], [v]
        for s in range(2):
            keys.append(kv_ref[:, s, :, c].reshape(t, HD))
            values.append(kv_ref[:, s, :, n + h * HD : n + (h + 1) * HD].reshape(t, HD))
        sc = [_nt(kk, q) * factor for kk in keys]
        key_at = lax.broadcasted_iota(jnp.int32, (t, t), 0)
        query_at = lax.broadcasted_iota(jnp.int32, (t, t), 1)
        sc[0] = jnp.where(key_at <= query_at, sc[0], -jnp.inf)
        m = functools.reduce(jnp.maximum, [jnp.max(x, axis=0, keepdims=True) for x in sc])
        e = [jnp.exp(x - m) for x in sc]
        il = 1.0 / sum(jnp.sum(x, axis=0, keepdims=True) for x in e)
        p = [x * il for x in e]
        low = [x.astype(BF) for x in p]
        dp = [_nt(vv, do) for vv in values]
        delta = sum(
            jnp.sum(a.astype(F32) * b, axis=0, keepdims=True) for a, b in zip(low, dp)
        )
        ds = [(a * (b - delta)).astype(BF) for a, b in zip(p, dp)]
        gq = sum(_tn(a, kk) for a, kk in zip(ds, keys)) * factor
        gq_ref[:, c] = gq.astype(BF)
        st_ref[3 * h : 3 * h + 1, :] = m
        st_ref[3 * h + 1 : 3 * h + 2, :] = il
        st_ref[3 * h + 2 : 3 * h + 3, :] = delta


def attend(factor, qkv, kv, after):
    t, n = qkv.shape
    n = n // 4
    return pl.pallas_call(
        functools.partial(_attend_body, factor),
        in_specs=[VMEM] * 2 + [ANY] * len(after),
        out_specs=[VMEM] * 2,
        out_shape=[
            jax.ShapeDtypeStruct((t, n), BF),
            jax.ShapeDtypeStruct((8, t), F32),
        ],
        compiler_params=_params(SMALL),
        cost_estimate=_cost(2 * 11 * t * t * n, 4 * t * n * 10, 3 * t * t * n // HD),
        name="attend",
    )(qkv, kv, *after)


def _settle_body(factor, p1_ref, p2_ref, qkv_ref, qdo_ref, *rest):
    gk_ref, gv_ref, both_ref = rest[-3:]
    st_refs = rest[:ZS]
    t, n = gk_ref.shape
    me = lax.axis_index("doc")
    names = [
        sum(jnp.where(p[d] == me, d, 0) for d in range(p1_ref.shape[0]))
        for p in (p1_ref, p2_ref)
    ]
    steps_z = [lax.rem(me // XS - d // XS + ZS, ZS) for d in names]
    steps_x = [lax.rem(lax.rem(me, XS) - lax.rem(d, XS) + XS, XS) for d in names]
    for h in range(n // HD):
        c = slice(h * HD, (h + 1) * HD)
        k = qkv_ref[:, n + h * HD : n + (h + 1) * HD]
        v = qkv_ref[:, 2 * n + h * HD : 2 * n + (h + 1) * HD]
        dk = dv = 0.0
        for s in range(3):
            if s == 2:
                st = st_refs[0][0]
                q, do = qkv_ref[:, c], qkv_ref[:, 3 * n + h * HD : 3 * n + (h + 1) * HD]
            else:
                st = st_refs[0][steps_x[s]]
                for j in range(1, ZS):
                    st = jnp.where(steps_z[s] == j, st_refs[j][steps_x[s]], st)
                q = qdo_ref[:, s, :, c].reshape(t, HD)
                do = qdo_ref[:, s, :, n + h * HD : n + (h + 1) * HD].reshape(t, HD)
            m, il, delta = (st[3 * h + i : 3 * h + i + 1, :] for i in range(3))
            sc = _nt(k, q) * factor
            if s == 2:
                key_at = lax.broadcasted_iota(jnp.int32, (t, t), 0)
                query_at = lax.broadcasted_iota(jnp.int32, (t, t), 1)
                sc = jnp.where(key_at <= query_at, sc, -jnp.inf)
            p = jnp.exp(sc - m) * il
            dp = _nt(v, do)
            ds = (p * (dp - delta)).astype(BF)
            dk = dk + _nn(ds, q) * factor
            dv = dv + _nn(p.astype(BF), do)
        gk, gv = dk.astype(BF), dv.astype(BF)
        gk_ref[:, c] = gk
        gv_ref[:, c] = gv
        both_ref[:, c] = gk
        both_ref[:, n + h * HD : n + (h + 1) * HD] = gv


def settle(factor, p1, p2, qkv, qdo, stats, after):
    t, n = qkv.shape
    n = n // 4
    return pl.pallas_call(
        functools.partial(_settle_body, factor),
        in_specs=[SMEM] * 2 + [VMEM] * (2 + ZS + len(after)),
        out_specs=[VMEM] * 3,
        out_shape=[
            jax.ShapeDtypeStruct((t, n), BF),
            jax.ShapeDtypeStruct((t, n), BF),
            jax.ShapeDtypeStruct((t, 2 * n), BF),
        ],
        compiler_params=_params(SMALL),
        cost_estimate=_cost(2 * 12 * t * t * n, 4 * t * n * 8, 3 * t * t * n // HD),
        name="settle",
    )(p1, p2, qkv, qdo, *stats, *after)


def _wgrad_body(flip, x_ref, *refs):
    gq, gkv, o_ref = refs[0:XS], refs[XS : 2 * XS], refs[2 * XS]
    half, n = o_ref.shape[1], gq[0].shape[1]
    core = lax.axis_index("cuts")
    if flip:
        core = 1 - core
    at = pl.multiple_of(core * half, half)
    xs = [
        jnp.concatenate([x_ref[k, :, pl.ds(z * 2 * half + at, half)] for z in range(ZS)], axis=1)
        for k in range(XS)
    ]
    for cols, gs in ((slice(0, n), gq), (slice(n, 2 * n), gkv), (slice(2 * n, 3 * n), gkv)):
        acc = None
        for x, g in zip(xs, gs):
            right = g[...] if gs is gq else g[:, cols.start - n : cols.stop - n]
            part = _tn(x, right)
            acc = part if acc is None else acc + part
        for z in range(ZS):
            o_ref[z, :, cols] = acc[z * half : (z + 1) * half].astype(BF)


def wgrad(flip, xs, gq, gkv):
    _, t, rows = xs.shape
    n = gq[0].shape[1]
    return pl.pallas_call(
        functools.partial(_wgrad_body, flip),
        in_specs=[VMEM] * (1 + 2 * XS),
        out_specs=VMEM,
        out_shape=jax.ShapeDtypeStruct((ZS, rows // (2 * ZS), 3 * n), BF),
        compiler_params=_params(SMALL),
        cost_estimate=_cost(3 * XS * t * rows * 3 * n, 2 * XS * t * (rows + 3 * n) + 3 * rows * n),
        name="wgrad",
    )(xs, *gq, *gkv)


def _pair_body(keep_ref, got_ref, own_ref, *outs):
    my_z = lax.axis_index("doc") // XS
    own_ref[...] = keep_ref[my_z].astype(F32) + got_ref[my_z].astype(F32)
    for k, o_ref in enumerate(outs):
        to = lax.rem(my_z + k + 1, ZS)
        o_ref[...] = (keep_ref[to].astype(F32) + got_ref[to].astype(F32)).astype(BF)


def pair(keep, got):
    piece = keep.shape[1:]
    return pl.pallas_call(
        _pair_body,
        in_specs=[VMEM] * 2,
        out_specs=[VMEM] * ZS,
        out_shape=[jax.ShapeDtypeStruct(piece, F32)]
        + [jax.ShapeDtypeStruct(piece, BF)] * (ZS - 1),
        compiler_params=_params(SMALL),
        cost_estimate=_cost(8 * HINT // 30, 6 * keep.size),
        name="pair",
    )(keep, got)


def _xgrad_body(wq_ref, wk_ref, wv_ref, gq_ref, gkv_ref, *rest):
    o_ref = rest[-1]
    n = gq_ref.shape[1]
    block = o_ref.shape[2]
    rb = 256
    for y in range(YS):
        for half in range(2):
            for r in range(block // rb):
                at = (half * YS + y) * block + r * rb
                rows = slice(at, at + rb)
                acc = (
                    _nt(wq_ref[rows], gq_ref[...])
                    + _nt(wk_ref[rows], gkv_ref[:, :n])
                    + _nt(wv_ref[rows], gkv_ref[:, n:])
                )
                o_ref[y, half, r * rb : (r + 1) * rb] = acc.astype(BF)


def xgrad(wq, wk, wv, gq, gkv, after):
    d, n = wq.shape
    t = gq.shape[0]
    return pl.pallas_call(
        _xgrad_body,
        in_specs=[VMEM] * (5 + len(after)),
        out_specs=VMEM,
        out_shape=jax.ShapeDtypeStruct((YS, 2, d // (2 * YS), t), BF),
        compiler_params=_params(SMALL),
        cost_estimate=_cost(6 * t * d * n, 6 * d * n + 8 * t * n + 2 * d * t),
        name="xgrad",
    )(wq, wk, wv, gq, gkv, *after)


def _join_body(terms_ref, keep_ref, send_ref):
    mine = lax.axis_index("head") // YS
    for half, o_ref in ((mine, keep_ref), (1 - mine, send_ref)):
        acc = terms_ref[0, half].astype(F32)
        for y in range(1, YS):
            acc = acc + terms_ref[y, half].astype(F32)
        o_ref[...] = acc.astype(o_ref.dtype)


def join(terms):
    shape = terms.shape[2:]
    return pl.pallas_call(
        _join_body,
        in_specs=[VMEM],
        out_specs=[VMEM, VMEM],
        out_shape=[jax.ShapeDtypeStruct(shape, F32), jax.ShapeDtypeStruct(shape, BF)],
        compiler_params=_params(SMALL),
        cost_estimate=_cost(4 * HINT // 30, 2 * terms.size),
        name="join",
    )(terms)


def shift_x(v, k):
    pairs = [(z * XS + x, z * XS + (x + k) % XS) for z in range(ZS) for x in range(XS)]
    return lax.ppermute(v, "doc", pairs)


def shift_z(v, k):
    pairs = [(z * XS + x, ((z + k) % ZS) * XS + x) for z in range(ZS) for x in range(XS)]
    return lax.ppermute(v, "doc", pairs)


def shift_y(v, k):
    pairs = [(a * YS + y, a * YS + (y + k) % YS) for a in range(2) for y in range(YS)]
    return lax.ppermute(v, "head", pairs)


def swap_halves(v):
    pairs = [(a * YS + y, (1 - a) * YS + y) for a in range(2) for y in range(YS)]
    return lax.ppermute(v, "head", pairs)


def swap_cores(v):
    return lax.ppermute(v, "cuts", [(0, 1), (1, 0)])


ORDER = (1, 3, 2)


def per_device(
    inputs, weight_query, weight_key, weight_value, grad_output, partner_one, partner_two
):
    x = inputs[0, 0]
    do = grad_output[0, 0]
    t, d = x.shape
    n = weight_query.shape[1]
    factor = 1.0 / math.sqrt(HD)
    docs = lax.axis_size("doc")
    rows = t // docs
    p1, p2 = partner_one[0], partner_two[0]
    def spread(v):
        return lax.all_to_all(v, "doc", split_axis=0, concat_axis=0, tiled=True)

    qkvd, *cuts = project(x, weight_query, weight_key, weight_value, do)
    blocks = spread(qkvd.reshape(docs, rows, 4 * n))

    quarters = stack([shift_x(cuts[k], k) for k in range(1, XS)])
    columns = merge(cuts[0], [shift_y(quarters, j) if j else quarters for j in range(YS)])

    kv = spread(pick(_pick_kv_body, p1, p2, blocks, [quarters]))
    qdo = spread(pick(_pick_qdo_body, p1, p2, blocks, [columns]))
    gq, stats = attend(factor, qkvd, kv, [])
    weights = [weight_query, weight_key, weight_value]
    row = jnp.stack([shift_x(stats, k) if k else stats for k in range(XS)])
    all_stats = [shift_z(row, k) if k else row for k in range(ZS)]
    gq_x = {0: gq, **{k: shift_x(gq, k) for k in ORDER}}
    gk, gv, gkv = settle(factor, p1, p2, qkvd, qdo, all_stats, weights)
    gkv_x = {0: gkv, **{k: shift_x(gkv, k) for k in ORDER}}

    terms = xgrad(*weights, gq, gkv, [gq_x[k] for k in ORDER])
    groups = [[a * YS + y for y in range(YS)] for a in range(2)]
    terms = lax.all_to_all(
        terms, "head", split_axis=0, concat_axis=0, tiled=True, axis_index_groups=groups
    )
    operands = (columns, [gq_x[k] for k in range(XS)], [gkv_x[k] for k in range(XS)])
    theirs = wgrad(True, *operands)
    mine = wgrad(False, *operands)
    total, *pieces = pair(mine, swap_cores(theirs))
    for k in range(1, ZS):
        total = total + shift_z(pieces[k - 1], k).astype(F32)
    keep, send = join(terms)
    features = (keep + swap_halves(send).astype(F32)).astype(BF)
    return (
        gk.reshape(1, 1, t, n),
        gv.reshape(1, 1, t, n),
        total[:, :n],
        total[:, n : 2 * n],
        total[:, 2 * n :],
        features.reshape(1, 1, features.shape[0], t),
    )


def solution(mesh):
    in_specs = (
        P("cuts", "doc", None, None),
        P(None, "head"),
        P(None, "head"),
        P(None, "head"),
        P("cuts", "doc", None, "head"),
        P("cuts", None),
        P("cuts", None),
    )
    out_specs = (
        P("cuts", "doc", None, "head"),
        P("cuts", "doc", None, "head"),
        P(("doc", "cuts"), "head"),
        P(("doc", "cuts"), "head"),
        P(("doc", "cuts"), "head"),
        P("cuts", "doc", "head", None),
    )
    return jax.shard_map(
        per_device, mesh=mesh, in_specs=in_specs, out_specs=out_specs, check_vma=False
    )
```

```python
import functools
import math

import jax
import jax.numpy as jnp
from jax import lax
from jax.experimental import pallas as pl
from jax.experimental.pallas import tpu as pltpu
from jax.sharding import PartitionSpec as P

HD = 128
XS = 4
ZS = 4
YS = 4
BF = jnp.bfloat16
F32 = jnp.float32
SMALL = 16 * 1024 * 1024
LARGE = 52 * 1024 * 1024
VMEM = pl.BlockSpec(memory_space=pltpu.VMEM)
SMEM = pl.BlockSpec(memory_space=pltpu.SMEM)
ANY = pl.BlockSpec(memory_space=pl.ANY)
HBM = pl.BlockSpec(memory_space=pltpu.HBM)


def _params(limit):
    return pltpu.CompilerParams(vmem_limit_bytes=limit)


def _cost(flops, nbytes, trans=0):
    return pl.CostEstimate(flops=flops, bytes_accessed=nbytes, transcendentals=trans)


def _nt(a, b):
    return lax.dot_general(a, b, (((1,), (1,)), ((), ())), preferred_element_type=F32)


def _nn(a, b):
    return lax.dot_general(a, b, (((1,), (0,)), ((), ())), preferred_element_type=F32)


def _tn(a, b):
    return lax.dot_general(a, b, (((0,), (0,)), ((), ())), preferred_element_type=F32)


PIECES = 8
HINT = 30_000_000_000


def _project_body(x_ref, wq_ref, wk_ref, wv_ref, do_ref, o_ref, *rest):
    outs, (xs, ws, acc, sems) = rest[:XS], rest[XS:]
    d, n = wq_ref.shape
    my_x = lax.rem(lax.axis_index("doc"), XS)
    width = d // (ZS * XS)
    kb = d // PIECES
    last = pltpu.make_async_copy(do_ref, o_ref.at[:, 3 * n :], sems.at[PIECES, 0])
    copies = []
    for i in range(PIECES):
        part = slice(i * kb, (i + 1) * kb)
        row = [pltpu.make_async_copy(x_ref.at[:, part], xs.at[:, part], sems.at[i, 0])]
        for j, w in enumerate((wq_ref, wk_ref, wv_ref)):
            row.append(pltpu.make_async_copy(w.at[part, :], ws.at[j, part, :], sems.at[i, j + 1]))
        for c in row:
            c.start()
        copies.append(row)
    last.start()
    for i in range(PIECES):
        part = slice(i * kb, (i + 1) * kb)
        for c in copies[i]:
            c.wait()
        x = xs[:, part]
        for j in range(3):
            cols = slice(j * n, (j + 1) * n)
            prod = _nn(x, ws[j, part, :])
            if i == 0:
                acc[:, cols] = prod
            elif i < PIECES - 1:
                acc[:, cols] += prod
            else:
                o_ref[:, cols] = (acc[:, cols] + prod).astype(BF)
    last.wait()
    quarter = xs.shape[0] // YS
    mine = pl.multiple_of(lax.rem(lax.axis_index("head"), YS) * quarter, quarter)
    for k in range(XS):
        rows = slice(None) if k == 0 else pl.ds(mine, quarter)
        for z in range(ZS):
            start = pl.multiple_of((z * XS + lax.rem(my_x + k, XS)) * width, width)
            outs[k][:, z * width : (z + 1) * width] = xs[rows, pl.ds(start, width)]


def project(x, wq, wk, wv, do):
    t, d = x.shape
    n = wq.shape[1]
    return pl.pallas_call(
        _project_body,
        in_specs=[ANY] * 5,
        out_specs=[VMEM] * (1 + XS),
        out_shape=[jax.ShapeDtypeStruct((t, 4 * n), BF)]
        + [jax.ShapeDtypeStruct((t if k == 0 else t // YS, d // XS), BF) for k in range(XS)],
        scratch_shapes=[
            pltpu.VMEM((t, d), BF),
            pltpu.VMEM((3, d, n), BF),
            pltpu.VMEM((t, 3 * n), F32),
            pltpu.SemaphoreType.DMA((PIECES + 1, 4)),
        ],
        compiler_params=_params(LARGE),
        cost_estimate=_cost(6 * t * d * n, 2 * (t * d + 3 * d * n)),
        name="project",
    )(x, wq, wk, wv, do)


def _stack_body(*refs):
    o_ref = refs[-1]
    for i, r in enumerate(refs[:-1]):
        o_ref[i] = r[...]


def stack(parts):
    shape = (len(parts), *parts[0].shape)
    return pl.pallas_call(
        _stack_body,
        in_specs=[VMEM] * len(parts),
        out_specs=VMEM,
        out_shape=jax.ShapeDtypeStruct(shape, BF),
        compiler_params=_params(SMALL),
        cost_estimate=_cost(HINT, 0),
        name="stack",
    )(*parts)


def _merge_body(own_ref, *refs):
    parts, o_ref = refs[:YS], refs[-1]
    quarter = parts[0].shape[1]
    my_y = lax.rem(lax.axis_index("head"), YS)
    o_ref[0] = own_ref[...]
    for j in range(YS):
        at = pl.multiple_of(lax.rem(my_y + YS - j, YS) * quarter, quarter)
        for k in range(1, XS):
            o_ref[k, pl.ds(at, quarter), :] = parts[j][k - 1]


def merge(own, parts):
    return pl.pallas_call(
        _merge_body,
        in_specs=[VMEM] * (1 + YS),
        out_specs=VMEM,
        out_shape=jax.ShapeDtypeStruct((XS, *own.shape), BF),
        compiler_params=_params(SMALL),
        cost_estimate=_cost(HINT, 0),
        name="merge",
    )(own, *parts)


def _pick_kv_body(p1_ref, p2_ref, all_ref, *rest):
    kv_ref = rest[-1]
    n = all_ref.shape[2] // 4

    def one(d, carry):
        for slot, p_ref in enumerate((p1_ref, p2_ref)):
            kv_ref[d, slot] = all_ref[p_ref[d], :, n : 3 * n]
        return carry

    lax.fori_loop(0, all_ref.shape[0], one, 0)


def _pick_qdo_body(p1_ref, p2_ref, all_ref, *rest):
    qdo_ref = rest[-1]
    n = all_ref.shape[2] // 4

    def one(d, carry):
        for slot, p_ref in enumerate((p1_ref, p2_ref)):
            p = p_ref[d]
            qdo_ref[p, slot, :, :n] = all_ref[d, :, :n]
            qdo_ref[p, slot, :, n:] = all_ref[d, :, 3 * n :]
        return carry

    lax.fori_loop(0, all_ref.shape[0], one, 0)


def pick(body, p1, p2, blocks, after):
    docs, rows, n = blocks.shape
    n = n // 4
    return pl.pallas_call(
        body,
        in_specs=[SMEM, SMEM, VMEM] + [VMEM] * len(after),
        out_specs=VMEM,
        out_shape=jax.ShapeDtypeStruct((docs, 2, rows, 2 * n), BF),
        compiler_params=_params(SMALL),
        cost_estimate=_cost(0, 2 * docs * rows * n * 8),
        name="pick",
    )(p1, p2, blocks, *after)


def _attend_body(factor, qkv_ref, kv_ref, *rest):
    gq_ref, st_ref = rest[-2:]
    t, n = gq_ref.shape
    st_ref[...] = jnp.zeros_like(st_ref)
    for h in range(n // HD):
        c = slice(h * HD, (h + 1) * HD)
        q = qkv_ref[:, c]
        k = qkv_ref[:, n + h * HD : n + (h + 1) * HD]
        v = qkv_ref[:, 2 * n + h * HD : 2 * n + (h + 1) * HD]
        do = qkv_ref[:, 3 * n + h * HD : 3 * n + (h + 1) * HD]
        keys, values = [k], [v]
        for s in range(2):
            keys.append(kv_ref[:, s, :, c].reshape(t, HD))
            values.append(kv_ref[:, s, :, n + h * HD : n + (h + 1) * HD].reshape(t, HD))
        sc = [_nt(kk, q) * factor for kk in keys]
        key_at = lax.broadcasted_iota(jnp.int32, (t, t), 0)
        query_at = lax.broadcasted_iota(jnp.int32, (t, t), 1)
        sc[0] = jnp.where(key_at <= query_at, sc[0], -jnp.inf)
        m = functools.reduce(jnp.maximum, [jnp.max(x, axis=0, keepdims=True) for x in sc])
        e = [jnp.exp(x - m) for x in sc]
        il = 1.0 / sum(jnp.sum(x, axis=0, keepdims=True) for x in e)
        p = [x * il for x in e]
        low = [x.astype(BF) for x in p]
        dp = [_nt(vv, do) for vv in values]
        delta = sum(
            jnp.sum(a.astype(F32) * b, axis=0, keepdims=True) for a, b in zip(low, dp)
        )
        ds = [(a * (b - delta)).astype(BF) for a, b in zip(p, dp)]
        gq = sum(_tn(a, kk) for a, kk in zip(ds, keys)) * factor
        gq_ref[:, c] = gq.astype(BF)
        st_ref[3 * h : 3 * h + 1, :] = m
        st_ref[3 * h + 1 : 3 * h + 2, :] = il
        st_ref[3 * h + 2 : 3 * h + 3, :] = delta


def attend(factor, qkv, kv, after):
    t, n = qkv.shape
    n = n // 4
    return pl.pallas_call(
        functools.partial(_attend_body, factor),
        in_specs=[VMEM] * 2 + [ANY] * len(after),
        out_specs=[VMEM] * 2,
        out_shape=[
            jax.ShapeDtypeStruct((t, n), BF),
            jax.ShapeDtypeStruct((8, t), F32),
        ],
        compiler_params=_params(SMALL),
        cost_estimate=_cost(2 * 11 * t * t * n, 4 * t * n * 10, 3 * t * t * n // HD),
        name="attend",
    )(qkv, kv, *after)


def _settle_body(factor, p1_ref, p2_ref, qkv_ref, qdo_ref, *rest):
    gk_ref, gv_ref, both_ref = rest[-3:]
    st_refs = rest[:ZS]
    t, n = gk_ref.shape
    me = lax.axis_index("doc")
    names = [
        sum(jnp.where(p[d] == me, d, 0) for d in range(p1_ref.shape[0]))
        for p in (p1_ref, p2_ref)
    ]
    steps_z = [lax.rem(me // XS - d // XS + ZS, ZS) for d in names]
    steps_x = [lax.rem(lax.rem(me, XS) - lax.rem(d, XS) + XS, XS) for d in names]
    for h in range(n // HD):
        c = slice(h * HD, (h + 1) * HD)
        k = qkv_ref[:, n + h * HD : n + (h + 1) * HD]
        v = qkv_ref[:, 2 * n + h * HD : 2 * n + (h + 1) * HD]
        dk = dv = 0.0
        for s in range(3):
            if s == 2:
                st = st_refs[0][0]
                q, do = qkv_ref[:, c], qkv_ref[:, 3 * n + h * HD : 3 * n + (h + 1) * HD]
            else:
                st = st_refs[0][steps_x[s]]
                for j in range(1, ZS):
                    st = jnp.where(steps_z[s] == j, st_refs[j][steps_x[s]], st)
                q = qdo_ref[:, s, :, c].reshape(t, HD)
                do = qdo_ref[:, s, :, n + h * HD : n + (h + 1) * HD].reshape(t, HD)
            m, il, delta = (st[3 * h + i : 3 * h + i + 1, :] for i in range(3))
            sc = _nt(k, q) * factor
            if s == 2:
                key_at = lax.broadcasted_iota(jnp.int32, (t, t), 0)
                query_at = lax.broadcasted_iota(jnp.int32, (t, t), 1)
                sc = jnp.where(key_at <= query_at, sc, -jnp.inf)
            p = jnp.exp(sc - m) * il
            dp = _nt(v, do)
            ds = (p * (dp - delta)).astype(BF)
            dk = dk + _nn(ds, q) * factor
            dv = dv + _nn(p.astype(BF), do)
        gk, gv = dk.astype(BF), dv.astype(BF)
        gk_ref[:, c] = gk
        gv_ref[:, c] = gv
        both_ref[:, c] = gk
        both_ref[:, n + h * HD : n + (h + 1) * HD] = gv


def settle(factor, p1, p2, qkv, qdo, stats, after):
    t, n = qkv.shape
    n = n // 4
    return pl.pallas_call(
        functools.partial(_settle_body, factor),
        in_specs=[SMEM] * 2 + [VMEM] * (2 + ZS + len(after)),
        out_specs=[VMEM] * 3,
        out_shape=[
            jax.ShapeDtypeStruct((t, n), BF),
            jax.ShapeDtypeStruct((t, n), BF),
            jax.ShapeDtypeStruct((t, 2 * n), BF),
        ],
        compiler_params=_params(SMALL),
        cost_estimate=_cost(2 * 12 * t * t * n, 4 * t * n * 8, 3 * t * t * n // HD),
        name="settle",
    )(p1, p2, qkv, qdo, *stats, *after)


def _wgrad_body(flip, x_ref, *refs):
    gq, gkv, o_ref = refs[0:XS], refs[XS : 2 * XS], refs[2 * XS]
    half, n = o_ref.shape[1], gq[0].shape[1]
    core = lax.axis_index("cuts")
    if flip:
        core = 1 - core
    at = pl.multiple_of(core * half, half)
    xs = [
        jnp.concatenate([x_ref[k, :, pl.ds(z * 2 * half + at, half)] for z in range(ZS)], axis=1)
        for k in range(XS)
    ]
    for cols, gs in ((slice(0, n), gq), (slice(n, 2 * n), gkv), (slice(2 * n, 3 * n), gkv)):
        acc = None
        for x, g in zip(xs, gs):
            right = g[...] if gs is gq else g[:, cols.start - n : cols.stop - n]
            part = _tn(x, right)
            acc = part if acc is None else acc + part
        for z in range(ZS):
            o_ref[z, :, cols] = acc[z * half : (z + 1) * half].astype(BF)


def wgrad(flip, xs, gq, gkv):
    _, t, rows = xs.shape
    n = gq[0].shape[1]
    return pl.pallas_call(
        functools.partial(_wgrad_body, flip),
        in_specs=[VMEM] * (1 + 2 * XS),
        out_specs=VMEM,
        out_shape=jax.ShapeDtypeStruct((ZS, rows // (2 * ZS), 3 * n), BF),
        compiler_params=_params(SMALL),
        cost_estimate=_cost(3 * XS * t * rows * 3 * n, 2 * XS * t * (rows + 3 * n) + 3 * rows * n),
        name="wgrad",
    )(xs, *gq, *gkv)


def _pair_body(keep_ref, got_ref, own_ref, *outs):
    my_z = lax.axis_index("doc") // XS
    own_ref[...] = keep_ref[my_z].astype(F32) + got_ref[my_z].astype(F32)
    for k, o_ref in enumerate(outs):
        to = lax.rem(my_z + k + 1, ZS)
        o_ref[...] = (keep_ref[to].astype(F32) + got_ref[to].astype(F32)).astype(BF)


def pair(keep, got):
    piece = keep.shape[1:]
    return pl.pallas_call(
        _pair_body,
        in_specs=[VMEM] * 2,
        out_specs=[VMEM] * ZS,
        out_shape=[jax.ShapeDtypeStruct(piece, F32)]
        + [jax.ShapeDtypeStruct(piece, BF)] * (ZS - 1),
        compiler_params=_params(SMALL),
        cost_estimate=_cost(8 * HINT // 30, 6 * keep.size),
        name="pair",
    )(keep, got)


def _xgrad_body(wq_ref, wk_ref, wv_ref, gq_ref, gkv_ref, *rest):
    o_ref = rest[-1]
    n = gq_ref.shape[1]
    block = o_ref.shape[2]
    rb = 256
    for y in range(YS):
        for half in range(2):
            for r in range(block // rb):
                at = (half * YS + y) * block + r * rb
                rows = slice(at, at + rb)
                acc = (
                    _nt(wq_ref[rows], gq_ref[...])
                    + _nt(wk_ref[rows], gkv_ref[:, :n])
                    + _nt(wv_ref[rows], gkv_ref[:, n:])
                )
                o_ref[y, half, r * rb : (r + 1) * rb] = acc.astype(BF)


def xgrad(wq, wk, wv, gq, gkv, after):
    d, n = wq.shape
    t = gq.shape[0]
    return pl.pallas_call(
        _xgrad_body,
        in_specs=[VMEM] * (5 + len(after)),
        out_specs=VMEM,
        out_shape=jax.ShapeDtypeStruct((YS, 2, d // (2 * YS), t), BF),
        compiler_params=_params(SMALL),
        cost_estimate=_cost(6 * t * d * n, 6 * d * n + 8 * t * n + 2 * d * t),
        name="xgrad",
    )(wq, wk, wv, gq, gkv, *after)


def _join_body(terms_ref, keep_ref, send_ref):
    mine = lax.axis_index("head") // YS
    for half, o_ref in ((mine, keep_ref), (1 - mine, send_ref)):
        acc = terms_ref[0, half].astype(F32)
        for y in range(1, YS):
            acc = acc + terms_ref[y, half].astype(F32)
        o_ref[...] = acc.astype(o_ref.dtype)


def join(terms):
    shape = terms.shape[2:]
    return pl.pallas_call(
        _join_body,
        in_specs=[VMEM],
        out_specs=[VMEM, VMEM],
        out_shape=[jax.ShapeDtypeStruct(shape, F32), jax.ShapeDtypeStruct(shape, BF)],
        compiler_params=_params(SMALL),
        cost_estimate=_cost(4 * HINT // 30, 2 * terms.size),
        name="join",
    )(terms)


def _finish_body(own_ref, a_ref, b_ref, c_ref, *outs):
    n = outs[0].shape[1]
    for i in range(3):
        cols = slice(i * n, (i + 1) * n)
        total = own_ref[:, cols]
        for r in (a_ref, b_ref, c_ref):
            total = total + r[:, cols].astype(F32)
        outs[i][...] = total


def finish(own, pieces):
    rows, n = own.shape
    return pl.pallas_call(
        _finish_body,
        in_specs=[VMEM] * 4,
        out_specs=[VMEM] * 3,
        out_shape=[jax.ShapeDtypeStruct((rows, n // 3), F32)] * 3,
        compiler_params=_params(SMALL),
        cost_estimate=_cost(4 * HINT // 30, 16 * own.size),
        name="finish",
    )(own, *pieces)


def shift_x(v, k):
    pairs = [(z * XS + x, z * XS + (x + k) % XS) for z in range(ZS) for x in range(XS)]
    return lax.ppermute(v, "doc", pairs)


def shift_z(v, k):
    pairs = [(z * XS + x, ((z + k) % ZS) * XS + x) for z in range(ZS) for x in range(XS)]
    return lax.ppermute(v, "doc", pairs)


def shift_y(v, k):
    pairs = [(a * YS + y, a * YS + (y + k) % YS) for a in range(2) for y in range(YS)]
    return lax.ppermute(v, "head", pairs)


def swap_halves(v):
    pairs = [(a * YS + y, (1 - a) * YS + y) for a in range(2) for y in range(YS)]
    return lax.ppermute(v, "head", pairs)


def swap_cores(v):
    return lax.ppermute(v, "cuts", [(0, 1), (1, 0)])


ORDER = (1, 3, 2)


def per_device(
    inputs, weight_query, weight_key, weight_value, grad_output, partner_one, partner_two
):
    x = inputs[0, 0]
    do = grad_output[0, 0]
    t, d = x.shape
    n = weight_query.shape[1]
    factor = 1.0 / math.sqrt(HD)
    docs = lax.axis_size("doc")
    rows = t // docs
    p1, p2 = partner_one[0], partner_two[0]
    def spread(v):
        return lax.all_to_all(v, "doc", split_axis=0, concat_axis=0, tiled=True)

    qkvd, *cuts = project(x, weight_query, weight_key, weight_value, do)
    blocks = spread(qkvd.reshape(docs, rows, 4 * n))

    quarters = stack([shift_x(cuts[k], k) for k in range(1, XS)])
    columns = merge(cuts[0], [shift_y(quarters, j) if j else quarters for j in range(YS)])

    kv = spread(pick(_pick_kv_body, p1, p2, blocks, [quarters]))
    qdo = spread(pick(_pick_qdo_body, p1, p2, blocks, [columns]))
    gq, stats = attend(factor, qkvd, kv, [])
    weights = [weight_query, weight_key, weight_value]
    row = jnp.stack([shift_x(stats, k) if k else stats for k in range(XS)])
    all_stats = [shift_z(row, k) if k else row for k in range(ZS)]
    gq_x = {0: gq, **{k: shift_x(gq, k) for k in ORDER}}
    gk, gv, gkv = settle(factor, p1, p2, qkvd, qdo, all_stats, [])
    gkv_x = {0: gkv, **{k: shift_x(gkv, k) for k in ORDER}}

    terms = xgrad(*weights, gq, gkv, [gq_x[k] for k in ORDER])
    groups = [[a * YS + y for y in range(YS)] for a in range(2)]
    terms = lax.all_to_all(
        terms, "head", split_axis=0, concat_axis=0, tiled=True, axis_index_groups=groups
    )
    operands = (columns, [gq_x[k] for k in range(XS)], [gkv_x[k] for k in range(XS)])
    theirs = wgrad(True, *operands)
    mine = wgrad(False, *operands)
    total, *pieces = pair(mine, swap_cores(theirs))
    gwq, gwk, gwv = finish(total, [shift_z(pieces[k - 1], k) for k in range(1, ZS)])
    keep, send = join(terms)
    features = (keep + swap_halves(send).astype(F32)).astype(BF)
    return (
        gk.reshape(1, 1, t, n),
        gv.reshape(1, 1, t, n),
        gwq,
        gwk,
        gwv,
        features.reshape(1, 1, features.shape[0], t),
    )


def solution(mesh):
    in_specs = (
        P("cuts", "doc", None, None),
        P(None, "head"),
        P(None, "head"),
        P(None, "head"),
        P("cuts", "doc", None, "head"),
        P("cuts", None),
        P("cuts", None),
    )
    out_specs = (
        P("cuts", "doc", None, "head"),
        P("cuts", "doc", None, "head"),
        P(("doc", "cuts"), "head"),
        P(("doc", "cuts"), "head"),
        P(("doc", "cuts"), "head"),
        P("cuts", "doc", "head", None),
    )
    return jax.shard_map(
        per_device, mesh=mesh, in_specs=in_specs, out_specs=out_specs, check_vma=False
    )
```
